512 devices in a mesh: con: 8 (over x_lo, y), slab: 64 (over x_hi, z, core).
Axes of the slice: x: 4 (x_hi: 2, x_lo: 2; x = x_hi * 2 + x_lo), y: 4, z: 16, core: 2. Of those that a mesh axis runs over, the one named last changes fastest.
Arguments:
- image: float32 [8, 2, 2, 320, 320], P('con', None, None, 'slab'), may hold values from -6 to 6
- dual: float32 [8, 6, 2, 320, 320], P('con', None, None, 'slab'), may hold values from -4 to 4
- adjoint_data: float32 [8, 2, 2, 320, 320], P('con', None, None, 'slab'), may hold values from -6 to 6
- sens: float32 [8, 2, 2, 320, 320], P(None, None, None, 'slab'), may hold values from -2 to 2
- kern: float32 [8, 640, 640], P('con', 'slab'), may hold values from 0.05 to 2
Outputs:
- new_image: float32 [8, 2, 2, 320, 320], P('con', None, None, 'slab')
- new_dual: float32 [8, 6, 2, 320, 320], P('con', None, None, 'slab')
The draws below stay inside these ranges and needn't reach their ends.
All inputs are finite; a program needn't handle non-finite values.
Results may differ from the reference program's by a relative error of at most 0.00005.
Values sent between devices are 32-bit elements; how exact they have to be, the bound alone decides.
No kernel may reach another device: no remote copies, remote signals or barrier semaphores. Data moves between devices by JAX's collectives and lax.ppermute only.
A program may use at most 64 MiB of HBM per device.

```python
import math
import jax
import jax.numpy as jnp
from jax import lax

NX = 320
NY = 320
COILS = 8
ZW = 2
CONTRASTS = 8


def level_of(own_key, dims, pieces, low, high):
    def one(position, parts):
        draws = jax.random.uniform(jax.random.fold_in(jax.random.fold_in(own_key, 6), position), (parts,), jnp.float32, low / len(pieces), high / len(pieces))
        return jnp.repeat(jnp.exp(draws), dims[position] // parts).reshape((-1,) + (1,) * (len(dims) - position - 1))

    factor_of = one(*pieces[0])
    for cut in pieces[1:]:
        factor_of = factor_of * one(*cut)
    return factor_of


def gaussian(key, dims, width, most, shards=(), held_as=jnp.bfloat16):
    level = level_of(key, dims, shards, -0.22, 0.18) if shards else 1.0
    result = jax.random.normal(key, dims, jnp.float32) * width * level
    return jnp.minimum(jnp.maximum(result, -most), most).astype(held_as)


def setup_inputs(seed: int = 0) -> dict:
    seeds = jax.random.split(jax.random.key(seed), 6)
    return {
        "image": gaussian(seeds[0], (CONTRASTS, 2, ZW, NX, NY), 1.0, 6.0, ((0, 8), (3, 64)), jnp.float32),
        "dual": gaussian(seeds[1], (CONTRASTS, 6, ZW, NX, NY), 0.5, 4.0, ((0, 8), (3, 64)), jnp.float32),
        "adjoint_data": gaussian(seeds[2], (CONTRASTS, 2, ZW, NX, NY), 1.0, 6.0, ((0, 8), (3, 64)), jnp.float32),
        "sens": gaussian(seeds[3], (COILS, 2, ZW, NX, NY), 0.35, 2.0, ((3, 64),), jnp.float32),
        "kern": jnp.clip(jnp.exp(math.log(2.0) - 3.6888794 * jax.random.uniform(seeds[4], (CONTRASTS, 2 * NY, 2 * NX), jnp.float32) ** level_of(seeds[4], (CONTRASTS, 2 * NY, 2 * NX), ((0, 8), (1, 64)), -0.2, 0.2)), 0.05, 2.0),
    }


def normal_op(field, sens, kern_one):
    image_c = lax.complex(field[0], field[1])
    sens_c = lax.complex(sens[:, 0], sens[:, 1])
    coil_image = sens_c * image_c[None]
    spectrum = jnp.fft.fft2(coil_image, s=(2 * NX, 2 * NY), axes=(2, 3))
    weighted = spectrum * kern_one.T[None, None]
    returned = jnp.fft.ifft2(weighted, axes=(2, 3))[:, :, :NX, :NY]
    total = lax.optimization_barrier(jnp.sum(jnp.conj(sens_c) * returned, axis=0))
    return jnp.stack([jnp.real(total), jnp.imag(total)]).astype(field.dtype)

def forward_diff(field, axis):
    steps_along = jnp.diff(field, axis=axis)
    edge = jnp.zeros_like(lax.slice_in_dim(field, 0, 1, axis=axis))
    return jnp.concatenate([steps_along, edge], axis=axis)

def adjoint_diff(field, axis):
    length = field.shape[axis]
    shape = [1] * field.ndim
    shape[axis] = length
    inner = (jnp.arange(length) < length - 1).astype(field.dtype).reshape(shape)
    masked = field * inner
    edge = jnp.zeros_like(lax.slice_in_dim(field, 0, 1, axis=axis))
    before = jnp.concatenate([edge, lax.slice_in_dim(masked, 0, length - 1, axis=axis)], axis=axis)
    return before - masked

def reference(image, dual, adjoint_data, sens, kern):
    normal = jnp.stack([normal_op(image[c], sens, kern[c]) for c in range(CONTRASTS)])
    adjoint_grad = adjoint_diff(dual[:, 0:2], 3) + adjoint_diff(dual[:, 2:4], 4) + adjoint_diff(dual[:, 4:6], 2)
    new_image = image - 0.2 * (normal - adjoint_data + adjoint_grad)
    extra = 2.0 * new_image - image
    grads = jnp.concatenate([forward_diff(extra, 3), forward_diff(extra, 4), forward_diff(extra, 2)], axis=1)
    moved = dual + 0.5 * grads
    energy = lax.optimization_barrier(jnp.sum(moved * moved, axis=(0, 1)))
    limit = 0.9 * jnp.sqrt(6.0 * CONTRASTS)
    factor = jnp.maximum(1.0, jnp.sqrt(energy) / limit)
    return (new_image, moved / factor[None, None])
```

```python
import functools
import math

import jax
import jax.numpy as jnp
import ml_dtypes
import numpy as np
from jax import lax
from jax.experimental import pallas as pl
from jax.experimental.pallas import tpu as pltpu
from jax.sharding import PartitionSpec as P

FULL = 320
PADDED = 640
SLABS = 64
ROWS = 5
BAND = 10
COILS = 8
PLANES = 2
PIECE = 2 * PLANES * COILS
TILES = 13
LANES = 128


def tile_of(x, b):
    if b < 8:
        return 2 * x + b // 4, b % 4
    return 10 + x // 2, (x % 2) * 2 + b - 8


def split(value):
    high = value.astype(jnp.bfloat16)
    return high, (value - high.astype(jnp.float32)).astype(jnp.bfloat16)


def np_split(value):
    high = value.astype(np.float32).astype(ml_dtypes.bfloat16)
    low = (value - high.astype(np.float64)).astype(np.float32).astype(ml_dtypes.bfloat16)
    return high, low


@functools.cache
def tables():
    order = np.arange(BAND)[:, None] + BAND * np.arange(SLABS)[None, :]
    k2 = order.reshape(-1)
    place = (np.arange(ROWS)[:, None] + ROWS * np.arange(SLABS)[None, :]).reshape(-1)
    k1 = np.arange(PADDED)
    y = np.arange(FULL)
    turn_y = 2 * np.pi * (k2[:, None] * y[None, :] % PADDED) / PADDED
    turn_x = 2 * np.pi * (k1[:, None] * place[None, :] % PADDED) / PADDED
    cos_y, sin_y = np.cos(turn_y), np.sin(turn_y)
    cos_x, sin_x = np.cos(turn_x), np.sin(turn_x)
    forward_x = np.concatenate([cos_x, sin_x], axis=1)
    back_x = np.concatenate([cos_x.T, sin_x.T], axis=0)
    gap = ((0, 384 - FULL), (0, 0))
    back_y = np.concatenate([np.pad(cos_y.T, gap), np.pad(sin_y.T, gap)], axis=0) / PADDED**2
    spread = np.zeros((BAND, 384), np.float32)
    for b in range(BAND):
        spread[b, b * PIECE : (b + 1) * PIECE] = 1.0
    first = (*np_split(cos_y), *np_split(sin_y))
    second = (*np_split(forward_x), *np_split(back_x), spread.astype(ml_dtypes.bfloat16))
    third = np_split(back_y)
    return first, second, third


def dot(left, right, transposed=False):
    form = (((1,), (1 if transposed else 0,)), ((), ()))
    return lax.dot_general(left, right, form, preferred_element_type=jnp.float32)


def dot3(left_high, left_low, right, transposed=False):
    high, low = split(right)
    return (
        dot(left_high, high, transposed)
        + dot(left_high, low, transposed)
        + dot(left_low, high, transposed)
    )


def group_of_lane(rows):
    return lax.broadcasted_iota(jnp.int32, (rows, LANES), 1) // 32


def turn(value, shift):
    shift %= LANES
    return value if shift == 0 else pltpu.roll(value, shift, 1)


def gather_pieces(sources, groups):
    result = None
    for at, source in enumerate(sources):
        if source is None:
            continue
        moved = turn(source[0], 32 * (at - source[1]))
        result = moved if result is None else jnp.where(groups == at, moved, result)
    return result


def swap_parts(value):
    rows = value.shape[0]
    is_real = lax.broadcasted_iota(jnp.int32, (rows, LANES), 1) % 32 < 16
    parts = []
    for at in range(0, value.shape[1], LANES):
        tile = value[:, at : at + LANES]
        parts.append(jnp.where(is_real, turn(tile, -16), turn(tile, 16)))
    return jnp.concatenate(parts, axis=1), jnp.concatenate([is_real] * len(parts), axis=1)


def first_kernel(image_ref, sens_ref, ch_ref, cl_ref, sh_ref, sl_ref, out_ref, rows_ref):
    for x in range(ROWS):
        for part in range(2):
            for z in range(PLANES):
                for j in range(COILS):
                    row = x * PIECE + part * 16 + z * 8 + j
                    rows_ref[row : row + 1, :] = sens_ref[j, part, z, x : x + 1, :]
    direct, crossed = [], []
    for x in range(ROWS):
        real, imag = [], []
        for z in range(PLANES):
            sr = rows_ref[x * PIECE + z * 8 : x * PIECE + z * 8 + 8, :]
            si = rows_ref[x * PIECE + 16 + z * 8 : x * PIECE + 16 + z * 8 + 8, :]
            ur = image_ref[0, 0, z, x : x + 1, :]
            ui = image_ref[0, 1, z, x : x + 1, :]
            real.append(sr * ur - si * ui)
            imag.append(sr * ui + si * ur)
        direct += real + imag
        crossed += imag + [-part for part in real]
    rest = jnp.zeros((256 - ROWS * PIECE, FULL), jnp.float32)
    direct = jnp.concatenate(direct + [rest], axis=0)
    crossed = jnp.concatenate(crossed + [rest], axis=0)
    bands = dot3(ch_ref[...], cl_ref[...], direct, True) + dot3(
        sh_ref[...], sl_ref[...], crossed, True
    )
    groups = group_of_lane(SLABS)
    wanted = [[None] * 4 for _ in range(TILES)]
    for x in range(ROWS):
        for b in range(BAND):
            tile, at = tile_of(x, b)
            column = x // 4 * LANES
            wanted[tile][at] = (
                bands[b * SLABS : (b + 1) * SLABS, column : column + LANES],
                x % 4,
            )
    for tile in range(TILES):
        out_ref[pl.ds(tile, SLABS, stride=TILES), :] = gather_pieces(wanted[tile], groups)


def second_kernel(in_ref, kern_ref, fh_ref, fl_ref, bh_ref, bl_ref, spread_ref, out_ref):
    def tile(t):
        return in_ref[pl.ds(t, SLABS, stride=TILES), :]

    rows = []
    for x in range(ROWS):
        rest = turn(tile(10 + x // 2), -64 * (x % 2))
        rows.append(jnp.concatenate([tile(2 * x), tile(2 * x + 1), rest], axis=1))
    data = jnp.concatenate(rows, axis=0)
    swapped, is_real = swap_parts(data)
    data = jnp.concatenate([data, jnp.where(is_real, swapped, -swapped)], axis=0)
    spectrum = dot3(fh_ref[...], fl_ref[...], data)
    kern_high, kern_low = split(kern_ref[0])
    form = (((0,), (0,)), ((), ()))
    weight = lax.dot_general(
        kern_high, spread_ref[...], form, preferred_element_type=jnp.float32
    ) + lax.dot_general(kern_low, spread_ref[...], form, preferred_element_type=jnp.float32)
    both = dot3(bh_ref[...], bl_ref[...], spectrum * weight)
    swapped, is_real = swap_parts(both[FULL:])
    result = both[:FULL] + jnp.where(is_real, -swapped, swapped)
    lower = lax.broadcasted_iota(jnp.int32, (SLABS, LANES), 1) < 64
    for x in range(ROWS):
        for g in range(2):
            out_ref[pl.ds(2 * x + g, SLABS, stride=TILES), :] = result[
                x * SLABS : (x + 1) * SLABS, g * LANES : (g + 1) * LANES
            ]
    for pair in range(3):
        rest = result[2 * pair * SLABS : (2 * pair + 1) * SLABS, 256:384]
        if pair < 2:
            other = result[(2 * pair + 1) * SLABS : (2 * pair + 2) * SLABS, 256:384]
            rest = jnp.where(lower, rest, turn(other, 64))
        out_ref[pl.ds(10 + pair, SLABS, stride=TILES), :] = rest


def third_kernel(in_ref, rows_ref, th_ref, tl_ref, normal_ref):
    def tile(t):
        return in_ref[pl.ds(t, SLABS, stride=TILES), :]

    groups = group_of_lane(SLABS)
    bands = []
    for b in range(BAND):
        pieces = []
        for x in range(ROWS):
            t, at = tile_of(x, b)
            pieces.append((tile(t), at))
        columns = [gather_pieces(pieces[:4], groups), gather_pieces(pieces[4:], groups)]
        bands.append(jnp.concatenate(columns, axis=1))
    both = dot3(th_ref[...], tl_ref[...], jnp.concatenate(bands, axis=0))
    swapped, is_real = swap_parts(both[384:])
    back = (both[:384] + jnp.where(is_real, -swapped, swapped)).T
    for x in range(ROWS):
        for z in range(PLANES):
            at = x * PIECE + z * 8
            sr = rows_ref[at : at + 8, :]
            si = rows_ref[at + 16 : at + 24, :]
            br = back[at : at + 8, :FULL]
            bi = back[at + 16 : at + 24, :FULL]
            normal_ref[0, z, x : x + 1, :] = jnp.sum(sr * br + si * bi, axis=0, keepdims=True)
            normal_ref[1, z, x : x + 1, :] = jnp.sum(sr * bi - si * br, axis=0, keepdims=True)


PARAMS = pltpu.CompilerParams(vmem_limit_bytes=40 * 2**20)


def exchange(value):
    blocks = value.reshape(SLABS, 1, TILES * LANES)
    return lax.all_to_all(blocks, "slab", 0, 0, tiled=True).reshape(SLABS * TILES, LANES)


def normal_image(image, sens, kern):
    first, second, third = tables()
    block = jax.ShapeDtypeStruct((SLABS * TILES, LANES), jnp.float32)
    bands, sens_rows = pl.pallas_call(
        first_kernel,
        out_shape=(block, jax.ShapeDtypeStruct((ROWS * PIECE, FULL), jnp.float32)),
        compiler_params=PARAMS,
        name="first",
    )(image, sens, *first)
    returned = pl.pallas_call(
        second_kernel, out_shape=block, compiler_params=PARAMS, name="second"
    )(exchange(bands), kern, *second)
    return pl.pallas_call(
        third_kernel,
        out_shape=jax.ShapeDtypeStruct((2, PLANES, ROWS, FULL), jnp.float32),
        compiler_params=PARAMS,
        name="third",
    )(exchange(returned), sens_rows, *third)


def shifted(value, axis, by):
    count = lax.axis_size(axis)
    pairs = [(i, i + by) for i in range(count) if 0 <= i + by < count]
    return lax.ppermute(value, axis, pairs)


def local_forward(field, axis):
    length = field.shape[axis]
    steps_along = lax.slice_in_dim(field, 1, length, axis=axis) - lax.slice_in_dim(
        field, 0, length - 1, axis=axis
    )
    edge = jnp.zeros_like(lax.slice_in_dim(field, 0, 1, axis=axis))
    return jnp.concatenate([steps_along, edge], axis=axis)


def local_adjoint(field, axis):
    length = field.shape[axis]
    shape = [1] * field.ndim
    shape[axis] = length
    inner = (jnp.arange(length) < length - 1).astype(jnp.float32).reshape(shape)
    masked = field * inner
    edge = jnp.zeros_like(lax.slice_in_dim(field, 0, 1, axis=axis))
    before = jnp.concatenate([edge, lax.slice_in_dim(masked, 0, length - 1, axis=axis)], axis=axis)
    return before - masked


def total_over(value, axis):
    count = lax.axis_size(axis)
    copies = jnp.broadcast_to(value[None], (count, *value.shape))
    return jnp.sum(lax.all_to_all(copies, axis, 0, 0, tiled=True), axis=0)


def local(image, dual, adjoint_data, sens, kern):
    field = image[0]
    dual_now = dual[0]
    measured = adjoint_data[0]
    slab_count = lax.axis_size("slab")
    local_x = field.shape[2]
    full_x = local_x * slab_count
    global_x = lax.axis_index("slab") * local_x + jnp.arange(local_x, dtype=jnp.int32)
    inner_x = (global_x < full_x - 1).astype(jnp.float32)[None, None, :, None]
    rim_dual = shifted(dual_now[0:2, :, local_x - 1 :, :], "slab", 1)
    masked_x = dual_now[0:2] * inner_x
    adjoint_x = jnp.concatenate([rim_dual, masked_x[:, :, : local_x - 1]], axis=2) - masked_x
    adjoint_grad = adjoint_x + local_adjoint(dual_now[2:4], 3) + local_adjoint(dual_now[4:6], 1)
    normal = normal_image(image, sens, kern)
    new_field = field - 0.2 * (normal - measured + adjoint_grad)
    extra = 2.0 * new_field - field
    rim_image = shifted(extra[:, :, :1, :], "slab", -1)
    grad_x = (jnp.concatenate([extra[:, :, 1:], rim_image], axis=2) - extra) * inner_x
    grads = jnp.concatenate([grad_x, local_forward(extra, 3), local_forward(extra, 1)], axis=0)
    moved = dual_now + 0.5 * grads
    energy = total_over(jnp.sum(moved * moved, axis=0), "con")
    contrasts = lax.axis_size("con") * image.shape[0]
    limit = 0.9 * math.sqrt(6.0 * contrasts)
    factor = jnp.maximum(1.0, jnp.sqrt(energy) / limit)
    new_dual = moved / factor[None]
    return (new_field[None], new_dual[None])


def solution(mesh):
    return jax.shard_map(
        local,
        mesh=mesh,
        in_specs=(
            P("con", None, None, "slab", None),
            P("con", None, None, "slab", None),
            P("con", None, None, "slab", None),
            P(None, None, None, "slab", None),
            P("con", "slab", None),
        ),
        out_specs=(P("con", None, None, "slab", None), P("con", None, None, "slab", None)),
        check_vma=False,
    )
```

```python
import functools
import math

import jax
import jax.numpy as jnp
import ml_dtypes
import numpy as np
from jax import lax
from jax.experimental import pallas as pl
from jax.experimental.pallas import tpu as pltpu
from jax.sharding import PartitionSpec as P

FULL = 320
PADDED = 640
QUARTER = 160
SLABS = 64
ROWS = 5
BAND = 10
COILS = 8
PLANES = 2
PIECE = 2 * PLANES * COILS
TILES = 13
LANES = 128


def tile_of(x, b):
    if b < 8:
        return 2 * x + b // 4, b % 4
    return 10 + x // 2, (x % 2) * 2 + b - 8


def split(value):
    high = value.astype(jnp.bfloat16)
    return high, (value - high.astype(jnp.float32)).astype(jnp.bfloat16)


def np_split(value):
    high = value.astype(np.float32).astype(ml_dtypes.bfloat16)
    low = (value - high.astype(np.float64)).astype(np.float32).astype(ml_dtypes.bfloat16)
    return high, low


@functools.cache
def tables():
    low = np.arange(QUARTER)
    by_band = (np.arange(BAND)[:, None] + BAND * np.arange(16)[None, :]).reshape(-1)
    points_y = [4 * np.arange(80) + r for r in range(4)]
    points_x = []
    for r in range(4):
        order = [5 * (4 * u + (r - x) % 4) + x for x in range(ROWS) for u in range(16)]
        points_x.append(np.array(order))

    def stack(points, k):
        result = []
        for point in points:
            angle = 2 * np.pi * (k[:, None] * point[None, :] % PADDED) / PADDED
            result.append(np.concatenate([np.cos(angle), np.sin(angle)], axis=1))
        return np.stack(result)

    along_y = stack(points_y, by_band)
    along_x = stack(points_x, low)
    back_x = along_x.transpose(0, 2, 1)
    back_y = along_y.transpose(0, 2, 1) / PADDED**2
    spread = np.zeros((BAND, 384), np.float32)
    for b in range(BAND):
        spread[b, b * PIECE : (b + 1) * PIECE] = 1.0
    first = np.stack(np_split(along_y))
    second = np.stack(np_split(along_x) + np_split(back_x))
    third = np.stack(np_split(back_y))
    return first, second, third, spread.astype(ml_dtypes.bfloat16)


def dot(left, right):
    return jnp.dot(left, right, preferred_element_type=jnp.float32)


def dot3(left_high, left_low, right):
    high, low = split(right)
    return dot(left_high, high) + dot(left_high, low) + dot(left_low, high)


def turn(value, shift):
    shift %= LANES
    return value if shift == 0 else pltpu.roll(value, shift, 1)


def gather_pieces(sources, groups):
    result = None
    for at, source in enumerate(sources):
        if source is None:
            continue
        moved = turn(source[0], 32 * (at - source[1]))
        result = moved if result is None else jnp.where(groups == at, moved, result)
    return result


def times_minus_i(value):
    rows = value.shape[0]
    is_real = lax.broadcasted_iota(jnp.int32, (rows, LANES), 1) % 32 < 16
    parts = []
    for at in range(0, value.shape[1], LANES):
        tile = value[:, at : at + LANES]
        parts.append(jnp.where(is_real, turn(tile, -16), -turn(tile, 16)))
    return jnp.concatenate(parts, axis=1)


def butterfly(a0, a1, a2, a3):
    even, odd = a0 + a2, a1 + a3
    apart, turned = a0 - a2, times_minus_i(a1 - a3)
    return even + odd, apart + turned, even - odd, apart - turned


def forward(high_ref_of, low_ref_of, residues):
    parts = []
    for r in range(4):
        data = jnp.concatenate([residues[r], times_minus_i(residues[r])], axis=0)
        parts.append(dot3(high_ref_of(r), low_ref_of(r), data))
    return butterfly(*parts)


def backward(high_ref_of, low_ref_of, quarters):
    sums = butterfly(*quarters)
    result = []
    for r, at in enumerate((0, 3, 2, 1)):
        both = dot3(high_ref_of(r), low_ref_of(r), sums[at])
        result.append(both[:80] - times_minus_i(both[80:]))
    return result


def first_kernel(image_hbm, sens_hbm, table_hbm, out_ref, rows_ref, image_ref, sens_ref, table_ref, flat_ref, sems):
    copies = [
        pltpu.make_async_copy(sens_hbm, sens_ref, sems.at[0]),
        pltpu.make_async_copy(image_hbm, image_ref, sems.at[1]),
        pltpu.make_async_copy(table_hbm.at[0], table_ref.at[0], sems.at[2]),
        pltpu.make_async_copy(table_hbm.at[1], table_ref.at[1], sems.at[3]),
    ]
    for copy in copies:
        copy.start()
    copies[0].wait()
    for x in range(ROWS):
        for part in range(2):
            for j in range(COILS):
                row = x * PIECE + part * 16 + 2 * j
                rows_ref[row : row + 2, :] = sens_ref[j, part, x]
    copies[1].wait()
    coil = []
    for x in range(ROWS):
        sr = rows_ref[x * PIECE : x * PIECE + 16, :]
        si = rows_ref[x * PIECE + 16 : x * PIECE + 32, :]
        ur = jnp.concatenate([image_ref[0, 0, x]] * 8, axis=0)
        ui = jnp.concatenate([image_ref[0, 1, x]] * 8, axis=0)
        coil += [sr * ur - si * ui, sr * ui + si * ur]
    coil = jnp.concatenate(coil + [jnp.zeros((256 - ROWS * PIECE, FULL), jnp.float32)], axis=0)
    coil = jnp.concatenate([coil, jnp.zeros((256, 384 - FULL), jnp.float32)], axis=1).T
    flat_ref[0] = coil[:, :LANES]
    flat_ref[1] = coil[:, LANES:]
    residues = []
    for r in range(4):
        columns = [flat_ref[column, pl.ds(r, 80, stride=4), :] for column in range(2)]
        residues.append(jnp.concatenate(columns, axis=1))
    copies[2].wait()
    copies[3].wait()
    bands = forward(lambda r: table_ref[0, r], lambda r: table_ref[1, r], residues)
    groups = lax.broadcasted_iota(jnp.int32, (16, LANES), 1) // 32
    for q in range(4):
        wanted = [[None] * 4 for _ in range(TILES)]
        for x in range(ROWS):
            for b in range(BAND):
                tile, at = tile_of(x, b)
                column = x // 4 * LANES
                value = bands[q][b * 16 : (b + 1) * 16, column : column + LANES]
                wanted[tile][at] = (value, x % 4)
        for tile in range(TILES):
            out_ref[pl.ds(16 * q * TILES + tile, 16, stride=TILES), :] = gather_pieces(
                wanted[tile], groups
            )


def weight_kernel(kern_ref, spread_ref, out_ref):
    form = (((0,), (0,)), ((), ()))
    high, low = split(kern_ref[0])
    out_ref[...] = lax.dot_general(
        high, spread_ref[...], form, preferred_element_type=jnp.float32
    ) + lax.dot_general(low, spread_ref[...], form, preferred_element_type=jnp.float32)


def second_kernel(in_ref, weight_ref, table_ref, out_ref):
    def place(x, r, t):
        return pl.ds((r - x) % 4 * TILES + t, 16, stride=4 * TILES)

    residues = []
    for r in range(4):
        rows = []
        for x in range(ROWS):
            rest = turn(in_ref[place(x, r, 10 + x // 2), :], -64 * (x % 2))
            whole = [in_ref[place(x, r, 2 * x), :], in_ref[place(x, r, 2 * x + 1), :]]
            rows.append(jnp.concatenate(whole + [rest], axis=1))
        residues.append(jnp.concatenate(rows, axis=0))
    spectrum = forward(lambda r: table_ref[0, r], lambda r: table_ref[1, r], residues)
    weighted = [
        part * weight_ref[q * QUARTER : (q + 1) * QUARTER, :] for q, part in enumerate(spectrum)
    ]
    result = backward(lambda r: table_ref[2, r], lambda r: table_ref[3, r], weighted)
    for r in range(4):
        for x in range(ROWS):
            for g in range(2):
                out_ref[place(x, r, 2 * x + g), :] = result[r][
                    x * 16 : (x + 1) * 16, g * LANES : (g + 1) * LANES
                ]
    lower = lax.broadcasted_iota(jnp.int32, (16, LANES), 1) < 64
    for s in range(4):
        for pair in range(3):
            x = 2 * pair
            rest = result[(s + x) % 4][x * 16 : (x + 1) * 16, 256:384]
            if pair < 2:
                other = result[(s + x + 1) % 4][(x + 1) * 16 : (x + 2) * 16, 256:384]
                rest = jnp.where(lower, rest, turn(other, 64))
            out_ref[place(x, s + x, 10 + pair), :] = rest


def third_kernel(in_ref, rows_ref, table_ref, normal_ref, flat_ref):
    groups = lax.broadcasted_iota(jnp.int32, (16, LANES), 1) // 32
    quarters = []
    for q in range(4):
        tiles = [in_ref[pl.ds(16 * q * TILES + t, 16, stride=TILES), :] for t in range(TILES)]
        bands = []
        for b in range(BAND):
            pieces = []
            for x in range(ROWS):
                t, at = tile_of(x, b)
                pieces.append((tiles[t], at))
            columns = [gather_pieces(pieces[:4], groups), gather_pieces(pieces[4:], groups)]
            bands.append(jnp.concatenate(columns, axis=1))
        quarters.append(jnp.concatenate(bands, axis=0))
    back = backward(lambda r: table_ref[0, r], lambda r: table_ref[1, r], quarters)
    flat_ref[:, FULL:, :] = jnp.zeros((2, 384 - FULL, LANES), jnp.float32)
    for r in range(4):
        for column in range(2):
            flat_ref[column, pl.ds(r, 80, stride=4), :] = back[r][
                :, column * LANES : (column + 1) * LANES
            ]
    back = jnp.concatenate([flat_ref[0].T, flat_ref[1].T], axis=0)[:, :FULL]

    def over_coils(value):
        half = value[:8] + value[8:]
        quarter = half[:4] + half[4:]
        return quarter[:2] + quarter[2:]

    for x in range(ROWS):
        at = x * PIECE
        sr, si = rows_ref[at : at + 16, :], rows_ref[at + 16 : at + 32, :]
        br, bi = back[at : at + 16], back[at + 16 : at + 32]
        normal_ref[0, x] = over_coils(sr * br + si * bi)
        normal_ref[1, x] = over_coils(sr * bi - si * br)


PARAMS = pltpu.CompilerParams(vmem_limit_bytes=32 * 2**20)


def exchange(value):
    blocks = value.reshape(SLABS, 1, TILES * LANES)
    return lax.all_to_all(blocks, "slab", 0, 0, tiled=True).reshape(SLABS * TILES, LANES)


def normal_image(image, sens, kern):
    first, second, third, spread = tables()
    block = jax.ShapeDtypeStruct((SLABS * TILES, LANES), jnp.float32)
    weight = pl.pallas_call(
        weight_kernel,
        out_shape=jax.ShapeDtypeStruct((PADDED, 384), jnp.float32),
        compiler_params=PARAMS,
        name="weights",
    )(kern, spread)
    whole = pl.BlockSpec(memory_space=pltpu.HBM)
    bands, sens_rows = pl.pallas_call(
        first_kernel,
        in_specs=[whole] * 3,
        out_shape=(block, jax.ShapeDtypeStruct((ROWS * PIECE, FULL), jnp.float32)),
        scratch_shapes=[
            pltpu.VMEM(image.shape, jnp.float32),
            pltpu.VMEM(sens.shape, jnp.float32),
            pltpu.VMEM(first.shape, jnp.bfloat16),
            pltpu.VMEM((2, 384, LANES), jnp.float32),
            pltpu.SemaphoreType.DMA((4,)),
        ],
        compiler_params=pltpu.CompilerParams(vmem_limit_bytes=56*2**20),
        name="first",
    )(image, sens, first)
    returned = pl.pallas_call(
        second_kernel, out_shape=block, compiler_params=PARAMS, name="second"
    )(exchange(bands), weight, second)
    return pl.pallas_call(
        third_kernel,
        out_shape=jax.ShapeDtypeStruct((2, ROWS, PLANES, FULL), jnp.float32),
        scratch_shapes=[pltpu.VMEM((2, 384, LANES), jnp.float32)],
        compiler_params=PARAMS,
        name="third",
    )(exchange(returned), sens_rows, third)


def shifted(value, axis, by):
    count = lax.axis_size(axis)
    pairs = [(i, i + by) for i in range(count) if 0 <= i + by < count]
    return lax.ppermute(value, axis, pairs)


def local_forward(field, axis):
    length = field.shape[axis]
    steps_along = lax.slice_in_dim(field, 1, length, axis=axis) - lax.slice_in_dim(
        field, 0, length - 1, axis=axis
    )
    edge = jnp.zeros_like(lax.slice_in_dim(field, 0, 1, axis=axis))
    return jnp.concatenate([steps_along, edge], axis=axis)


def local_adjoint(field, axis):
    length = field.shape[axis]
    shape = [1] * field.ndim
    shape[axis] = length
    inner = (jnp.arange(length) < length - 1).astype(jnp.float32).reshape(shape)
    masked = field * inner
    edge = jnp.zeros_like(lax.slice_in_dim(field, 0, 1, axis=axis))
    before = jnp.concatenate([edge, lax.slice_in_dim(masked, 0, length - 1, axis=axis)], axis=axis)
    return before - masked


def total_over(value, axis):
    count = lax.axis_size(axis)
    copies = jnp.broadcast_to(value[None], (count, *value.shape))
    return jnp.sum(lax.all_to_all(copies, axis, 0, 0, tiled=True), axis=0)


def local(image, dual, adjoint_data, sens, kern):
    image, dual, adjoint_data, sens = (
        jnp.swapaxes(value, 2, 3) for value in (image, dual, adjoint_data, sens)
    )
    field = image[0]
    dual_now = dual[0]
    measured = adjoint_data[0]
    slab_count = lax.axis_size("slab")
    local_x = field.shape[1]
    full_x = local_x * slab_count
    global_x = lax.axis_index("slab") * local_x + jnp.arange(local_x, dtype=jnp.int32)
    inner_x = (global_x < full_x - 1).astype(jnp.float32)[None, :, None, None]
    rim_dual = shifted(dual_now[0:2, local_x - 1 :], "slab", 1)
    masked_x = dual_now[0:2] * inner_x
    adjoint_x = jnp.concatenate([rim_dual, masked_x[:, : local_x - 1]], axis=1) - masked_x
    adjoint_grad = adjoint_x + local_adjoint(dual_now[2:4], 3) + local_adjoint(dual_now[4:6], 2)
    normal = normal_image(image, sens, kern)
    new_field = field - 0.2 * (normal - measured + adjoint_grad)
    extra = 2.0 * new_field - field
    rim_image = shifted(extra[:, :1], "slab", -1)
    grad_x = (jnp.concatenate([extra[:, 1:], rim_image], axis=1) - extra) * inner_x
    grads = jnp.concatenate([grad_x, local_forward(extra, 3), local_forward(extra, 2)], axis=0)
    moved = dual_now + 0.5 * grads
    energy = total_over(jnp.sum(moved * moved, axis=0), "con")
    contrasts = lax.axis_size("con") * image.shape[0]
    limit = 0.9 * math.sqrt(6.0 * contrasts)
    factor = jnp.maximum(1.0, jnp.sqrt(energy) / limit)
    new_dual = moved / factor[None]
    return (jnp.swapaxes(new_field[None], 2, 3), jnp.swapaxes(new_dual[None], 2, 3))


def solution(mesh):
    return jax.shard_map(
        local,
        mesh=mesh,
        in_specs=(
            P("con", None, None, "slab", None),
            P("con", None, None, "slab", None),
            P("con", None, None, "slab", None),
            P(None, None, None, "slab", None),
            P("con", "slab", None),
        ),
        out_specs=(P("con", None, None, "slab", None), P("con", None, None, "slab", None)),
        check_vma=False,
    )
```

```python
import functools
import math

import jax
import jax.numpy as jnp
import ml_dtypes
import numpy as np
from jax import lax
from jax.experimental import pallas as pl
from jax.experimental.pallas import tpu as pltpu
from jax.sharding import PartitionSpec as P

FULL = 320
PADDED = 640
QUARTER = 160
SLABS = 64
ROWS = 5
BAND = 10
COILS = 8
PLANES = 2
PIECE = 2 * PLANES * COILS
TILES = 13
BACK_TILES = 15
LANES = 128
WIDE = 384


def tile_of(x, b, rows):
    if b < 8:
        return 2 * x + b // 4, b % 4
    return 2 * rows + x // 2, (x % 2) * 2 + b - 8


def split(value):
    high = value.astype(jnp.bfloat16)
    return high, (value - high.astype(jnp.float32)).astype(jnp.bfloat16)


def np_split(value):
    high = value.astype(np.float32).astype(ml_dtypes.bfloat16)
    low = (value - high.astype(np.float64)).astype(np.float32).astype(ml_dtypes.bfloat16)
    return high, low


@functools.cache
def tables():
    low = np.arange(QUARTER)
    by_band = (np.arange(BAND)[:, None] + BAND * np.arange(16)[None, :]).reshape(-1)
    points_y = [4 * np.arange(80) + r for r in range(4)]
    points_x = []
    for r in range(4):
        order = [5 * (4 * u + (r - x) % 4) + x for x in range(ROWS) for u in range(16)]
        points_x.append(np.array(order))

    def stack(points, k):
        result = []
        for point in points:
            angle = 2 * np.pi * (k[:, None] * point[None, :] % PADDED) / PADDED
            result.append(np.concatenate([np.cos(angle), np.sin(angle)], axis=1))
        return np.stack(result)

    along_y = stack(points_y, by_band)
    along_x = stack(points_x, low)
    back_x = along_x.transpose(0, 2, 1)
    back_y = along_y.transpose(0, 2, 1) / PADDED**2
    spread = np.zeros((BAND, WIDE), np.float32)
    for b in range(BAND):
        spread[b, b * PIECE : (b + 1) * PIECE] = 1.0
    first = np.stack(np_split(along_y))
    second = np.stack(np_split(along_x) + np_split(back_x))
    third = np.stack(np_split(back_y))
    return first, second, third, spread.astype(ml_dtypes.bfloat16)


def dot(left, right):
    return jnp.dot(left, right, preferred_element_type=jnp.float32)


def dot3(left_high, left_low, right):
    high, low = split(right)
    return dot(left_high, high) + dot(left_high, low) + dot(left_low, high)


def turn(value, shift):
    shift %= LANES
    return value if shift == 0 else pltpu.roll(value, shift, 1)


def gather_pieces(sources, groups):
    result = None
    for at, source in enumerate(sources):
        if source is None:
            continue
        moved = turn(source[0], 32 * (at - source[1]))
        result = moved if result is None else jnp.where(groups == at, moved, result)
    return result


def times_minus_i(value):
    rows = value.shape[0]
    is_real = lax.broadcasted_iota(jnp.int32, (rows, LANES), 1) % 32 < 16
    parts = []
    for at in range(0, value.shape[1], LANES):
        tile = value[:, at : at + LANES]
        parts.append(jnp.where(is_real, turn(tile, -16), -turn(tile, 16)))
    return jnp.concatenate(parts, axis=1)


def butterfly(a0, a1, a2, a3):
    even, odd = a0 + a2, a1 + a3
    apart, turned = a0 - a2, times_minus_i(a1 - a3)
    return even + odd, apart + turned, even - odd, apart - turned


def forward(high_ref_of, low_ref_of, residues):
    parts = []
    for r in range(4):
        data = jnp.concatenate([residues[r], times_minus_i(residues[r])], axis=0)
        parts.append(dot3(high_ref_of(r), low_ref_of(r), data))
    return butterfly(*parts)


def backward(high_ref_of, low_ref_of, quarters):
    sums = butterfly(*quarters)
    result = []
    for r, at in enumerate((0, 3, 2, 1)):
        both = dot3(high_ref_of(r), low_ref_of(r), sums[at])
        result.append(both[:80] - times_minus_i(both[80:]))
    return result


def first_kernel(image_hbm, sens_hbm, table_hbm, out_ref, rows_ref, image_ref, sens_ref, table_ref, flat_ref, sems):
    copies = [
        pltpu.make_async_copy(sens_hbm, sens_ref, sems.at[0]),
        pltpu.make_async_copy(image_hbm, image_ref, sems.at[1]),
        pltpu.make_async_copy(table_hbm.at[0], table_ref.at[0], sems.at[2]),
        pltpu.make_async_copy(table_hbm.at[1], table_ref.at[1], sems.at[3]),
    ]
    for copy in copies:
        copy.start()
    copies[0].wait()
    for x in range(ROWS):
        for part in range(2):
            for j in range(COILS):
                row = x * PIECE + part * 16 + 2 * j
                rows_ref[row : row + 2, :] = sens_ref[j, part, x]
    copies[1].wait()
    coil = []
    for x in range(ROWS):
        sr = rows_ref[x * PIECE : x * PIECE + 16, :]
        si = rows_ref[x * PIECE + 16 : x * PIECE + 32, :]
        ur = jnp.concatenate([image_ref[0, 0, x]] * 8, axis=0)
        ui = jnp.concatenate([image_ref[0, 1, x]] * 8, axis=0)
        coil += [sr * ur - si * ui, sr * ui + si * ur]
    coil = jnp.concatenate(coil + [jnp.zeros((256 - ROWS * PIECE, FULL), jnp.float32)], axis=0)
    coil = jnp.concatenate([coil, jnp.zeros((256, 384 - FULL), jnp.float32)], axis=1).T
    flat_ref[0] = coil[:, :LANES]
    flat_ref[1] = coil[:, LANES:]
    residues = []
    for r in range(4):
        columns = [flat_ref[column, pl.ds(r, 80, stride=4), :] for column in range(2)]
        residues.append(jnp.concatenate(columns, axis=1))
    copies[2].wait()
    copies[3].wait()
    bands = forward(lambda r: table_ref[0, r], lambda r: table_ref[1, r], residues)
    groups = lax.broadcasted_iota(jnp.int32, (16, LANES), 1) // 32
    for q in range(4):
        wanted = [[None] * 4 for _ in range(TILES)]
        for x in range(ROWS):
            for b in range(BAND):
                tile, at = tile_of(x, b, ROWS)
                column = x // 4 * LANES
                value = bands[q][b * 16 : (b + 1) * 16, column : column + LANES]
                wanted[tile][at] = (value, x % 4)
        for tile in range(TILES):
            out_ref[pl.ds(16 * q * TILES + tile, 16, stride=TILES), :] = gather_pieces(
                wanted[tile], groups
            )


def weight_kernel(kern_ref, spread_ref, out_ref):
    form = (((0,), (0,)), ((), ()))
    high, low = split(kern_ref[0])
    out_ref[...] = lax.dot_general(
        high, spread_ref[...], form, preferred_element_type=jnp.float32
    ) + lax.dot_general(low, spread_ref[...], form, preferred_element_type=jnp.float32)


def edge_kernel(image_ref, measured_ref, dual_ref, sens_ref, edge_ref, rim_ref):
    for at, count, source in ((0, 2, image_ref), (2, 2, measured_ref), (4, 6, dual_ref)):
        for channel in range(count):
            edge_ref[at + channel, 0] = source[0, channel, 0]
    for j in range(COILS):
        for part in range(2):
            edge_ref[10 + 2 * j + part, 0] = sens_ref[j, part, 0]
    for part in range(2):
        rim_ref[part, 0] = dual_ref[0, part, ROWS - 1]


def second_kernel(in_ref, weight_ref, table_ref, out_ref):
    def place(x, r, t):
        return pl.ds((r - x) % 4 * TILES + t, 16, stride=4 * TILES)

    residues = []
    for r in range(4):
        rows = []
        for x in range(ROWS):
            rest = turn(in_ref[place(x, r, 10 + x // 2), :], -64 * (x % 2))
            whole = [in_ref[place(x, r, 2 * x), :], in_ref[place(x, r, 2 * x + 1), :]]
            rows.append(jnp.concatenate(whole + [rest], axis=1))
        residues.append(jnp.concatenate(rows, axis=0))
    spectrum = forward(lambda r: table_ref[0, r], lambda r: table_ref[1, r], residues)
    weighted = [
        part * weight_ref[q * QUARTER : (q + 1) * QUARTER, :] for q, part in enumerate(spectrum)
    ]
    result = backward(lambda r: table_ref[2, r], lambda r: table_ref[3, r], weighted)
    lower = lax.broadcasted_iota(jnp.int32, (16, LANES), 1) < 64
    for s in range(4):

        def put(t, value):
            out_ref[pl.ds(s * BACK_TILES + t, 16, stride=4 * BACK_TILES), :] = value

        rows = [result[(s + x) % 4][x * 16 : (x + 1) * 16] for x in range(ROWS)]
        following = result[(s + 1) % 4][:16]
        rows.append(pltpu.roll(following, 15, 0) if s == 3 else following)
        for x in range(ROWS + 1):
            for g in range(2):
                put(2 * x + g, rows[x][:, g * LANES : (g + 1) * LANES])
        for pair in range(3):
            left, right = rows[2 * pair][:, 256:384], rows[2 * pair + 1][:, 256:384]
            put(12 + pair, jnp.where(lower, left, turn(right, 64)))


def third_kernel(
    last_ref, in_ref, rows_ref, table_ref, image_ref, measured_ref, dual_ref, edge_ref, rim_ref,
    new_ref, moved_ref, energy_ref, flat_ref, next_ref, plain_ref,
):
    groups = lax.broadcasted_iota(jnp.int32, (16, LANES), 1) // 32
    quarters = []
    for q in range(4):
        start = 16 * q * BACK_TILES
        tiles = [in_ref[pl.ds(start + t, 16, stride=BACK_TILES), :] for t in range(BACK_TILES)]
        bands = []
        for b in range(BAND):
            pieces = []
            for x in range(ROWS + 1):
                t, at = tile_of(x, b, ROWS + 1)
                pieces.append((tiles[t], at))
            columns = [gather_pieces(pieces[:4], groups), gather_pieces(pieces[4:], groups)]
            bands.append(jnp.concatenate(columns, axis=1))
        quarters.append(jnp.concatenate(bands, axis=0))
    back = backward(lambda r: table_ref[0, r], lambda r: table_ref[1, r], quarters)
    flat_ref[:, FULL:, :] = jnp.zeros((2, WIDE - FULL, LANES), jnp.float32)
    for r in range(4):
        for column in range(2):
            flat_ref[column, pl.ds(r, 80, stride=4), :] = back[r][
                :, column * LANES : (column + 1) * LANES
            ]
    back = jnp.concatenate([flat_ref[0].T, flat_ref[1].T], axis=0)[:, :FULL]

    def over_coils(value):
        half = value[:8] + value[8:]
        quarter = half[:4] + half[4:]
        return quarter[:2] + quarter[2:]

    for part in range(2):
        plain_ref[12 + part, :2, :FULL] = rim_ref[part, 0]
        for j in range(COILS):
            row = part * 16 + 2 * j
            next_ref[row : row + 2, :] = edge_ref[10 + 2 * j + part, 0]
    for source, at, count in ((image_ref, 0, 2), (measured_ref, 2, 2), (dual_ref, 4, 6)):
        for channel in range(count):
            for x in range(ROWS):
                plain_ref[at + channel, 2 * x : 2 * x + 2, :FULL] = source[0, channel, x]
            plain_ref[at + channel, 2 * ROWS : 2 * ROWS + 2, :FULL] = edge_ref[at + channel, 0]
    for x in range(ROWS + 1):
        at = x * PIECE
        if x < ROWS:
            sr, si = rows_ref[at : at + 16, :], rows_ref[at + 16 : at + 32, :]
        else:
            sr, si = next_ref[:16, :], next_ref[16:, :]
        br, bi = back[at : at + 16], back[at + 16 : at + 32]
        plain_ref[10, 2 * x : 2 * x + 2, :FULL] = over_coils(sr * br + si * bi)
        plain_ref[11, 2 * x : 2 * x + 2, :FULL] = over_coils(sr * bi - si * br)

    row = lax.broadcasted_iota(jnp.int32, (16, WIDE), 0)
    lane = lax.broadcasted_iota(jnp.int32, (16, WIDE), 1)
    known = (lane < FULL) & (row < 2 * ROWS + 2)
    inner_y = lane < FULL - 1
    inner_z = row % 2 == 0
    inner_x = row < jnp.where(last_ref[0] > 0, 2 * ROWS - 2, 16)

    def field(at):
        return jnp.where(known, plain_ref[at], 0.0)

    moved = [None] * 6
    for part in range(2):
        own, across, through = field(4 + part), field(6 + part), field(8 + part)
        masked_x = jnp.where(inner_x, own, 0.0)
        masked_y = jnp.where(inner_y, across, 0.0)
        masked_z = jnp.where(inner_z, through, 0.0)
        before = jnp.where(row < 2, field(12 + part), pltpu.roll(masked_x, 2, 0))
        adjoint = (before - masked_x) + (pltpu.roll(masked_y, 1, 1) - masked_y)
        adjoint = adjoint + (pltpu.roll(masked_z, 1, 0) - masked_z)
        now = field(part)
        new = now - 0.2 * (field(10 + part) - field(2 + part) + adjoint)
        extra = 2.0 * new - now
        grad_x = jnp.where(inner_x, pltpu.roll(extra, 14, 0) - extra, 0.0)
        grad_y = jnp.where(inner_y, pltpu.roll(extra, WIDE - 1, 1) - extra, 0.0)
        grad_z = jnp.where(inner_z, pltpu.roll(extra, 15, 0) - extra, 0.0)
        moved[part] = own + 0.5 * grad_x
        moved[2 + part] = across + 0.5 * grad_y
        moved[4 + part] = through + 0.5 * grad_z
        for x in range(ROWS):
            new_ref[0, part, x] = new[2 * x : 2 * x + 2, :FULL]
    energy = sum(value * value for value in moved)
    for channel in range(6):
        moved_ref[channel] = moved[channel]
    for copy in range(energy_ref.shape[0]):
        energy_ref[copy] = energy


def last_kernel(limit, energy_ref, moved_ref, out_ref):
    energy = energy_ref[0]
    for at in range(1, energy_ref.shape[0]):
        energy = energy + energy_ref[at]
    factor = jnp.maximum(1.0, jnp.sqrt(energy) / limit)
    for channel in range(6):
        value = moved_ref[channel] / factor
        for x in range(ROWS):
            out_ref[0, channel, x] = value[2 * x : 2 * x + 2, :FULL]


PARAMS = pltpu.CompilerParams(vmem_limit_bytes=32 * 2**20)


def exchange(value):
    tiles = value.shape[0] // SLABS
    blocks = value.reshape(SLABS, 1, tiles * LANES)
    return lax.all_to_all(blocks, "slab", 0, 0, tiled=True).reshape(SLABS * tiles, LANES)


def shifted(value, axis, by):
    count = lax.axis_size(axis)
    pairs = [(i, i + by) for i in range(count) if 0 <= i + by < count]
    return lax.ppermute(value, axis, pairs)


def local(image, dual, adjoint_data, sens, kern):
    image, dual, adjoint_data, sens = (
        jnp.swapaxes(value, 2, 3) for value in (image, dual, adjoint_data, sens)
    )
    first, second, third, spread = tables()
    contrasts = lax.axis_size("con")
    weight = pl.pallas_call(
        weight_kernel,
        out_shape=jax.ShapeDtypeStruct((PADDED, WIDE), jnp.float32),
        compiler_params=PARAMS,
        name="weights",
    )(kern, spread)
    whole = pl.BlockSpec(memory_space=pltpu.HBM)
    bands, sens_rows = pl.pallas_call(
        first_kernel,
        in_specs=[whole] * 3,
        out_shape=(
            jax.ShapeDtypeStruct((SLABS * TILES, LANES), jnp.float32),
            jax.ShapeDtypeStruct((ROWS * PIECE, FULL), jnp.float32),
        ),
        scratch_shapes=[
            pltpu.VMEM(image.shape, jnp.float32),
            pltpu.VMEM(sens.shape, jnp.float32),
            pltpu.VMEM(first.shape, jnp.bfloat16),
            pltpu.VMEM((2, WIDE, LANES), jnp.float32),
            pltpu.SemaphoreType.DMA((4,)),
        ],
        compiler_params=pltpu.CompilerParams(vmem_limit_bytes=56 * 2**20),
        name="first",
    )(image, sens, first)
    edge, rim = pl.pallas_call(
        edge_kernel,
        out_shape=(
            jax.ShapeDtypeStruct((10 + 2 * COILS, 1, PLANES, FULL), jnp.float32),
            jax.ShapeDtypeStruct((2, 1, PLANES, FULL), jnp.float32),
        ),
        compiler_params=PARAMS,
        name="edge",
    )(image, adjoint_data, dual, sens)
    edge = shifted(edge, "slab", -1)
    rim = shifted(rim, "slab", 1)
    returned = pl.pallas_call(
        second_kernel,
        out_shape=jax.ShapeDtypeStruct((SLABS * BACK_TILES, LANES), jnp.float32),
        compiler_params=PARAMS,
        name="second",
    )(exchange(bands), weight, second)
    is_last = (lax.axis_index("slab") == SLABS - 1).astype(jnp.int32).reshape(1)
    plain = jax.ShapeDtypeStruct((6, 16, WIDE), jnp.float32)
    new_image, moved, energy = pl.pallas_call(
        third_kernel,
        in_specs=[pl.BlockSpec(memory_space=pltpu.SMEM)]
        + [pl.BlockSpec(memory_space=pltpu.VMEM)] * 8,
        out_shape=(
            jax.ShapeDtypeStruct(image.shape, jnp.float32),
            plain,
            jax.ShapeDtypeStruct((contrasts, 16, WIDE), jnp.float32),
        ),
        scratch_shapes=[
            pltpu.VMEM((2, WIDE, LANES), jnp.float32),
            pltpu.VMEM((PIECE, FULL), jnp.float32),
            pltpu.VMEM((14, 16, WIDE), jnp.float32),
        ],
        compiler_params=PARAMS,
        name="third",
    )(is_last, exchange(returned), sens_rows, third, image, adjoint_data, dual, edge, rim)
    new_dual = pl.pallas_call(
        functools.partial(last_kernel, 0.9 * math.sqrt(6.0 * contrasts)),
        out_shape=jax.ShapeDtypeStruct(dual.shape, jnp.float32),
        compiler_params=PARAMS,
        name="last",
    )(lax.all_to_all(energy, "con", 0, 0, tiled=True), moved)
    return jnp.swapaxes(new_image, 2, 3), jnp.swapaxes(new_dual, 2, 3)


def solution(mesh):
    return jax.shard_map(
        local,
        mesh=mesh,
        in_specs=(
            P("con", None, None, "slab", None),
            P("con", None, None, "slab", None),
            P("con", None, None, "slab", None),
            P(None, None, None, "slab", None),
            P("con", "slab", None),
        ),
        out_specs=(P("con", None, None, "slab", None), P("con", None, None, "slab", None)),
        check_vma=False,
    )
```

```python
import functools
import math

import jax
import jax.numpy as jnp
import ml_dtypes
import numpy as np
from jax import lax
from jax.experimental import pallas as pl
from jax.experimental.pallas import tpu as pltpu
from jax.sharding import PartitionSpec as P

FULL = 320
PADDED = 640
QUARTER = 160
SLABS = 64
ROWS = 5
BAND = 10
COILS = 8
PLANES = 2
PIECE = PLANES * COILS
TILES = 13
BACK_TILES = 15
LANES = 128
WIDE = 384


def tile_of(x, b, rows):
    if b < 8:
        return 2 * x + b // 4, b % 4
    return 2 * rows + x // 2, (x % 2) * 2 + b - 8


def split(value):
    high = value.astype(jnp.bfloat16)
    return high, (value - high.astype(jnp.float32)).astype(jnp.bfloat16)


def np_split(value):
    high = value.astype(np.float32).astype(ml_dtypes.bfloat16)
    low = (value - high.astype(np.float64)).astype(np.float32).astype(ml_dtypes.bfloat16)
    return high, low


@functools.cache
def tables():
    low = np.arange(QUARTER)
    by_band = (np.arange(BAND)[:, None] + BAND * np.arange(16)[None, :]).reshape(-1)
    points_y = [4 * np.arange(80) + r for r in range(4)]
    points_x = []
    for r in range(4):
        order = [5 * (4 * u + (r - x) % 4) + x for x in range(ROWS) for u in range(16)]
        points_x.append(np.array(order))

    def stack(points, k):
        result = []
        for point in points:
            angle = 2 * np.pi * (k[:, None] * point[None, :] % PADDED) / PADDED
            result.append(np.concatenate([np.cos(angle), np.sin(angle)], axis=1))
        return np.stack(result)

    along_y = stack(points_y, by_band)
    along_x = stack(points_x, low)
    back_x = along_x.transpose(0, 2, 1)
    back_y = along_y.transpose(0, 2, 1) / PADDED**2
    spread = np.zeros((BAND, WIDE), np.float32)
    for b in range(BAND):
        for part in range(2):
            at = b // 4 * LANES + part * 64 + b % 4 * PIECE
            spread[b, at : at + PIECE] = 1.0
    first = np.stack(np_split(along_y), axis=1)
    second = np.stack([np.concatenate([h, h, l], axis=2) for h, l in (np_split(along_x), np_split(back_x))])
    third = np.stack(np_split(back_y))
    return first, second, third, spread.astype(ml_dtypes.bfloat16)


def dot(left, right):
    return jnp.dot(left, right, preferred_element_type=jnp.float32)


def dot3(left_high, left_low, right):
    high, low = split(right)
    if right.shape[1] > 256:
        return dot(left_high, jnp.concatenate([high, low, high], axis=0))
    return dot(left_high, high) + dot(left_high, low) + dot(left_low, high)


def turn(value, shift):
    shift %= LANES
    return value if shift == 0 else pltpu.roll(value, shift, 1)


def slot_of_lane(rows):
    return lax.broadcasted_iota(jnp.int32, (rows, LANES), 1) % 64 // PIECE


def gather_pieces(sources, slots):
    result = None
    for at, source in enumerate(sources):
        if source is None:
            continue
        moved = turn(source[0], PIECE * (at - source[1]))
        result = moved if result is None else jnp.where(slots == at, moved, result)
    return result


def transpose_pieces(tiles, slots):
    result = list(tiles)
    for step in (1, 2):
        low = slots // step % 2 == 0
        for at in (0, 1) if step == 2 else (0, 2):
            left, right = result[at], result[at + step]
            result[at] = jnp.where(low, left, turn(right, PIECE * step))
            result[at + step] = jnp.where(low, turn(left, -PIECE * step), right)
    return result


def times_minus_i(value):
    rows = value.shape[0]
    is_real = lax.broadcasted_iota(jnp.int32, (rows, LANES), 1) < 64
    parts = []
    for at in range(0, value.shape[1], LANES):
        turned = turn(value[:, at : at + LANES], 64)
        parts.append(jnp.where(is_real, turned, -turned))
    return jnp.concatenate(parts, axis=1)


def butterfly(a0, a1, a2, a3):
    even, odd = a0 + a2, a1 + a3
    apart, turned = a0 - a2, times_minus_i(a1 - a3)
    return even + odd, apart + turned, even - odd, apart - turned


def forward(high_ref_of, low_ref_of, residues):
    parts = []
    for r in range(4):
        data = jnp.concatenate([residues[r], times_minus_i(residues[r])], axis=0)
        parts.append(dot3(high_ref_of(r), low_ref_of(r), data))
    return butterfly(*parts)


def backward(high_ref_of, low_ref_of, quarters):
    sums = butterfly(*quarters)
    result = []
    for r, at in enumerate((0, 3, 2, 1)):
        both = dot3(high_ref_of(r), low_ref_of(r), sums[at])
        result.append(both[:80] - times_minus_i(both[80:]))
    return result


def gather_rows(sens_ref, rows_ref):
    for x in range(ROWS):
        for part in range(2):
            for j in range(COILS):
                row = (2 * x + part) * PIECE + 2 * j
                rows_ref[row : row + 2, :] = sens_ref[j, part, x]


def first_kernel(
    image_hbm, sens_hbm, table_hbm, out_ref,
    image_ref, sens_ref, table_ref, flat_ref, rows_ref, sems,
):
    copies = [
        pltpu.make_async_copy(sens_hbm, sens_ref, sems.at[0]),
        pltpu.make_async_copy(image_hbm, image_ref, sems.at[1]),
    ]
    for r in range(4):
        copies.append(pltpu.make_async_copy(table_hbm.at[r], table_ref.at[r], sems.at[2 + r]))
    for copy in copies:
        copy.start()
    copies[0].wait()
    gather_rows(sens_ref, rows_ref)
    copies[1].wait()
    real, imag = [], []
    for x in range(ROWS):
        sr = rows_ref[2 * x * PIECE : (2 * x + 1) * PIECE, :]
        si = rows_ref[(2 * x + 1) * PIECE : (2 * x + 2) * PIECE, :]
        ur = jnp.concatenate([image_ref[0, 0, x]] * COILS, axis=0)
        ui = jnp.concatenate([image_ref[0, 1, x]] * COILS, axis=0)
        real.append(sr * ur - si * ui)
        imag.append(sr * ui + si * ur)
    rest = [jnp.zeros((3 * PIECE, FULL), jnp.float32)]
    coil = jnp.concatenate(real[:4] + imag[:4] + real[4:] + rest + imag[4:] + rest, axis=0)
    coil = jnp.concatenate([coil, jnp.zeros((256, WIDE - FULL), jnp.float32)], axis=1).T
    flat_ref[0] = coil[:, :LANES]
    flat_ref[1] = coil[:, LANES:]
    residues = []
    for r in range(4):
        columns = [flat_ref[column, pl.ds(r, 80, stride=4), :] for column in range(2)]
        residues.append(jnp.concatenate(columns, axis=1))

    for r in range(4):
        copies[2 + r].wait()

    def table(r, level):
        return table_ref[r, level]

    bands = forward(lambda r: table(r, 0), lambda r: table(r, 1), residues)
    slots = slot_of_lane(16)
    for q in range(4):
        start = 16 * q * TILES

        def put(t, value):
            out_ref[pl.ds(start + t, 16, stride=TILES), :] = value

        near = [bands[q][b * 16 : (b + 1) * 16, :LANES] for b in range(BAND)]
        far = [bands[q][b * 16 : (b + 1) * 16, LANES:] for b in range(BAND)]
        for g in range(2):
            for x, value in enumerate(transpose_pieces(near[4 * g : 4 * g + 4], slots)):
                put(2 * x + g, value)
            put(8 + g, gather_pieces([(far[4 * g + i], 0) for i in range(4)], slots))
        for pair in range(2):
            pieces = [(near[8 + i], 2 * pair + x) for x in range(2) for i in range(2)]
            put(10 + pair, gather_pieces(pieces, slots))
        put(12, gather_pieces([(far[8], 0), (far[9], 0)], slots))


def weight_kernel(kern_ref, spread_ref, out_ref):
    form = (((0,), (0,)), ((), ()))
    high, low = split(kern_ref[0])
    out_ref[...] = lax.dot_general(
        high, spread_ref[...], form, preferred_element_type=jnp.float32
    ) + lax.dot_general(low, spread_ref[...], form, preferred_element_type=jnp.float32)


def edge_kernel(image_ref, measured_ref, dual_ref, sens_ref, edge_ref, rim_ref, rows_ref):
    gather_rows(sens_ref, rows_ref)
    for at, count, source in ((0, 2, image_ref), (2, 2, measured_ref), (4, 6, dual_ref)):
        for channel in range(count):
            edge_ref[at + channel, 0] = source[0, channel, 0]
    for j in range(COILS):
        for part in range(2):
            edge_ref[10 + 2 * j + part, 0] = sens_ref[j, part, 0]
    for part in range(2):
        rim_ref[part, 0] = dual_ref[0, part, ROWS - 1]


def second_kernel(in_ref, weight_ref, table_ref, out_ref):
    def place(x, r, t):
        return pl.ds((r - x) % 4 * TILES + t, 16, stride=4 * TILES)

    residues = []
    for r in range(4):
        rows = []
        for x in range(ROWS):
            rest = turn(in_ref[place(x, r, 10 + x // 2), :], -2 * PIECE * (x % 2))
            whole = [in_ref[place(x, r, 2 * x), :], in_ref[place(x, r, 2 * x + 1), :]]
            rows.append(jnp.concatenate(whole + [rest], axis=1))
        residues.append(jnp.concatenate(rows, axis=0))
    spectrum = forward(lambda r: table_ref[0, r], lambda r: None, residues)
    weighted = [
        part * weight_ref[q * QUARTER : (q + 1) * QUARTER, :] for q, part in enumerate(spectrum)
    ]
    result = backward(lambda r: table_ref[1, r], lambda r: None, weighted)
    lower = slot_of_lane(16) < 2
    for s in range(4):

        def put(t, value):
            out_ref[pl.ds(s * BACK_TILES + t, 16, stride=4 * BACK_TILES), :] = value

        rows = [result[(s + x) % 4][x * 16 : (x + 1) * 16] for x in range(ROWS)]
        following = result[(s + 1) % 4][:16]
        rows.append(pltpu.roll(following, 15, 0) if s == 3 else following)
        for x in range(ROWS + 1):
            for g in range(2):
                put(2 * x + g, rows[x][:, g * LANES : (g + 1) * LANES])
        for pair in range(3):
            left, right = rows[2 * pair][:, 2 * LANES :], rows[2 * pair + 1][:, 2 * LANES :]
            put(12 + pair, jnp.where(lower, left, turn(right, 2 * PIECE)))


def third_kernel(
    last_ref, in_ref, rows_ref, table_ref, image_ref, measured_ref, dual_ref, edge_ref, rim_ref,
    moved_ref, energy_ref, flat_ref, next_ref, plain_ref,
):
    slots = slot_of_lane(16)
    quarters = []
    for q in range(4):
        start = 16 * q * BACK_TILES
        tiles = [in_ref[pl.ds(start + t, 16, stride=BACK_TILES), :] for t in range(BACK_TILES)]
        near, far = [], []
        for g in range(2):
            near += transpose_pieces([tiles[2 * x + g] for x in range(4)], slots)
            far += [gather_pieces([(tiles[8 + g], i), (tiles[10 + g], i)], slots) for i in range(4)]
        for i in range(2):
            near.append(gather_pieces([(tiles[12 + x // 2], x % 2 * 2 + i) for x in range(4)], slots))
            far.append(gather_pieces([(tiles[14], i), (tiles[14], 2 + i)], slots))
        columns = [jnp.concatenate(near, axis=0), jnp.concatenate(far, axis=0)]
        quarters.append(jnp.concatenate(columns, axis=1))
    back = backward(lambda r: table_ref[0, r], lambda r: table_ref[1, r], quarters)
    flat_ref[:, FULL:, :] = jnp.zeros((2, WIDE - FULL, LANES), jnp.float32)
    for r in range(4):
        for column in range(2):
            flat_ref[column, pl.ds(r, 80, stride=4), :] = back[r][
                :, column * LANES : (column + 1) * LANES
            ]
    back = jnp.concatenate([flat_ref[0].T, flat_ref[1].T], axis=0)[:, :FULL]

    def over_coils(value):
        half = value[:8] + value[8:]
        quarter = half[:4] + half[4:]
        return quarter[:2] + quarter[2:]

    for part in range(2):
        plain_ref[12 + part, :2, :FULL] = rim_ref[part, 0]
        for j in range(COILS):
            row = part * PIECE + 2 * j
            next_ref[row : row + 2, :] = edge_ref[10 + 2 * j + part, 0]
    for source, at, count in ((image_ref, 0, 2), (measured_ref, 2, 2), (dual_ref, 4, 6)):
        for channel in range(count):
            for x in range(ROWS):
                plain_ref[at + channel, 2 * x : 2 * x + 2, :FULL] = source[0, channel, x]
            plain_ref[at + channel, 2 * ROWS : 2 * ROWS + 2, :FULL] = edge_ref[at + channel, 0]
    for x in range(ROWS + 1):
        if x < ROWS:
            at = 2 * x * PIECE
            sr, si = rows_ref[at : at + PIECE, :], rows_ref[at + PIECE : at + 2 * PIECE, :]
        else:
            sr, si = next_ref[:PIECE, :], next_ref[PIECE:, :]
        at = x // 4 * LANES + x % 4 * PIECE
        br, bi = back[at : at + PIECE], back[at + 64 : at + 64 + PIECE]
        plain_ref[10, 2 * x : 2 * x + 2, :FULL] = over_coils(sr * br + si * bi)
        plain_ref[11, 2 * x : 2 * x + 2, :FULL] = over_coils(sr * bi - si * br)

    row = lax.broadcasted_iota(jnp.int32, (16, WIDE), 0)
    lane = lax.broadcasted_iota(jnp.int32, (16, WIDE), 1)
    known = (lane < FULL) & (row < 2 * ROWS + 2)
    inner_y = lane < FULL - 1
    inner_z = row % 2 == 0
    inner_x = row < jnp.where(last_ref[0] > 0, 2 * ROWS - 2, 16)

    def field(at):
        return jnp.where(known, plain_ref[at], 0.0)

    moved = [None] * 6
    for part in range(2):
        own, across, through = field(4 + part), field(6 + part), field(8 + part)
        masked_x = jnp.where(inner_x, own, 0.0)
        masked_y = jnp.where(inner_y, across, 0.0)
        masked_z = jnp.where(inner_z, through, 0.0)
        before = jnp.where(row < 2, field(12 + part), pltpu.roll(masked_x, 2, 0))
        adjoint = (before - masked_x) + (pltpu.roll(masked_y, 1, 1) - masked_y)
        adjoint = adjoint + (pltpu.roll(masked_z, 1, 0) - masked_z)
        now = field(part)
        new = now - 0.2 * (field(10 + part) - field(2 + part) + adjoint)
        extra = 2.0 * new - now
        grad_x = jnp.where(inner_x, pltpu.roll(extra, 14, 0) - extra, 0.0)
        grad_y = jnp.where(inner_y, pltpu.roll(extra, WIDE - 1, 1) - extra, 0.0)
        grad_z = jnp.where(inner_z, pltpu.roll(extra, 15, 0) - extra, 0.0)
        moved[part] = own + 0.5 * grad_x
        moved[2 + part] = across + 0.5 * grad_y
        moved[4 + part] = through + 0.5 * grad_z
        moved_ref[6 + part] = new
    energy = sum(value * value for value in moved)
    for channel in range(6):
        moved_ref[channel] = moved[channel]
    for copy in range(energy_ref.shape[0]):
        for t in range(3):
            energy_ref[copy, 10 * t : 10 * t + 10, :] = energy[:10, t * LANES : (t + 1) * LANES]


def last_kernel(limit, energy_ref, moved_ref, new_ref, out_ref):
    energy = energy_ref[0]
    for at in range(1, energy_ref.shape[0]):
        energy = energy + energy_ref[at]
    scale = 1.0 / jnp.maximum(1.0, jnp.sqrt(energy) / limit)
    scale = jnp.concatenate([scale[10 * t : 10 * t + 10] for t in range(3)], axis=1)
    for channel in range(6):
        value = moved_ref[channel][:10] * scale
        for x in range(ROWS):
            out_ref[0, channel, x] = value[2 * x : 2 * x + 2, :FULL]
    for part in range(2):
        for x in range(ROWS):
            new_ref[0, part, x] = moved_ref[6 + part, 2 * x : 2 * x + 2, :FULL]


PARAMS = pltpu.CompilerParams(vmem_limit_bytes=32 * 2**20)


def exchange(value):
    tiles = value.shape[0] // SLABS
    blocks = value.reshape(SLABS, 1, tiles * LANES)
    return lax.all_to_all(blocks, "slab", 0, 0, tiled=True).reshape(SLABS * tiles, LANES)


def shifted(value, axis, by):
    count = lax.axis_size(axis)
    pairs = [(i, i + by) for i in range(count) if 0 <= i + by < count]
    return lax.ppermute(value, axis, pairs)


def local(image, dual, adjoint_data, sens, kern):
    image, dual, adjoint_data, sens = (
        jnp.swapaxes(value, 2, 3) for value in (image, dual, adjoint_data, sens)
    )
    first, second, third, spread = tables()
    contrasts = lax.axis_size("con")
    weight = pl.pallas_call(
        weight_kernel,
        out_shape=jax.ShapeDtypeStruct((PADDED, WIDE), jnp.float32),
        compiler_params=PARAMS,
        name="weights",
    )(kern, spread)
    whole = pl.BlockSpec(memory_space=pltpu.HBM)
    bands = pl.pallas_call(
        first_kernel,
        in_specs=[whole] * 3,
        out_shape=jax.ShapeDtypeStruct((SLABS * TILES, LANES), jnp.float32),
        scratch_shapes=[
            pltpu.VMEM(image.shape, jnp.float32),
            pltpu.VMEM(sens.shape, jnp.float32),
            pltpu.VMEM(first.shape, jnp.bfloat16),
            pltpu.VMEM((2, WIDE, LANES), jnp.float32),
            pltpu.VMEM((2 * ROWS * PIECE, FULL), jnp.float32),
            pltpu.SemaphoreType.DMA((6,)),
        ],
        compiler_params=pltpu.CompilerParams(vmem_limit_bytes=56 * 2**20),
        name="first",
    )(image, sens, first)
    edge, rim, sens_rows = pl.pallas_call(
        edge_kernel,
        out_shape=(
            jax.ShapeDtypeStruct((10 + 2 * COILS, 1, PLANES, FULL), jnp.float32),
            jax.ShapeDtypeStruct((2, 1, PLANES, FULL), jnp.float32),
            jax.ShapeDtypeStruct((2 * ROWS * PIECE, FULL), jnp.float32),
        ),
        compiler_params=PARAMS,
        name="edge",
    )(image, adjoint_data, dual, sens)
    edge = shifted(edge, "slab", -1)
    rim = shifted(rim, "slab", 1)
    returned = pl.pallas_call(
        second_kernel,
        out_shape=jax.ShapeDtypeStruct((SLABS * BACK_TILES, LANES), jnp.float32),
        compiler_params=PARAMS,
        name="second",
    )(exchange(bands), weight, second)
    is_last = (lax.axis_index("slab") == SLABS - 1).astype(jnp.int32).reshape(1)
    moved, energy = pl.pallas_call(
        third_kernel,
        in_specs=[pl.BlockSpec(memory_space=pltpu.SMEM)]
        + [pl.BlockSpec(memory_space=pltpu.VMEM)] * 8,
        out_shape=(
            jax.ShapeDtypeStruct((8, 16, WIDE), jnp.float32),
            jax.ShapeDtypeStruct((contrasts, 30, LANES), jnp.float32),
        ),
        scratch_shapes=[
            pltpu.VMEM((2, WIDE, LANES), jnp.float32),
            pltpu.VMEM((2 * PIECE, FULL), jnp.float32),
            pltpu.VMEM((14, 16, WIDE), jnp.float32),
        ],
        compiler_params=PARAMS,
        name="third",
    )(is_last, exchange(returned), sens_rows, third, image, adjoint_data, dual, edge, rim)
    new_image, new_dual = pl.pallas_call(
        functools.partial(last_kernel, 0.9 * math.sqrt(6.0 * contrasts)),
        out_shape=(
            jax.ShapeDtypeStruct(image.shape, jnp.float32),
            jax.ShapeDtypeStruct(dual.shape, jnp.float32),
        ),
        compiler_params=PARAMS,
        name="last",
    )(lax.all_to_all(energy, "con", 0, 0, tiled=True), moved)
    return jnp.swapaxes(new_image, 2, 3), jnp.swapaxes(new_dual, 2, 3)


def solution(mesh):
    return jax.shard_map(
        local,
        mesh=mesh,
        in_specs=(
            P("con", None, None, "slab", None),
            P("con", None, None, "slab", None),
            P("con", None, None, "slab", None),
            P(None, None, None, "slab", None),
            P("con", "slab", None),
        ),
        out_specs=(P("con", None, None, "slab", None), P("con", None, None, "slab", None)),
        check_vma=False,
    )
```

```python
import functools
import math

import jax
import jax.numpy as jnp
import ml_dtypes
import numpy as np
from jax import lax
from jax.experimental import pallas as pl
from jax.experimental.pallas import tpu as pltpu
from jax.sharding import PartitionSpec as P

FULL = 320
PADDED = 640
QUARTER = 160
SLABS = 64
ROWS = 5
BAND = 10
COILS = 8
PLANES = 2
PIECE = PLANES * COILS
TILES = 13
BACK_TILES = 15
LANES = 128
WIDE = 384


def tile_of(x, b, rows):
    if b < 8:
        return 2 * x + b // 4, b % 4
    return 2 * rows + x // 2, (x % 2) * 2 + b - 8


def split(value):
    high = value.astype(jnp.bfloat16)
    return high, (value - high.astype(jnp.float32)).astype(jnp.bfloat16)


def np_split(value):
    high = value.astype(np.float32).astype(ml_dtypes.bfloat16)
    low = (value - high.astype(np.float64)).astype(np.float32).astype(ml_dtypes.bfloat16)
    return high, low


@functools.cache
def tables():
    low = np.arange(QUARTER)
    by_band = (np.arange(BAND)[:, None] + BAND * np.arange(16)[None, :]).reshape(-1)
    points_y = [4 * np.arange(80) + r for r in range(4)]
    points_x = []
    for r in range(4):
        order = [5 * (4 * u + (r - x) % 4) + x for x in range(ROWS) for u in range(16)]
        points_x.append(np.array(order))

    def stack(points, k):
        result = []
        for point in points:
            angle = 2 * np.pi * (k[:, None] * point[None, :] % PADDED) / PADDED
            result.append(np.concatenate([np.cos(angle), np.sin(angle)], axis=1))
        return np.stack(result)

    along_y = stack(points_y, by_band)
    along_x = stack(points_x, low)
    back_x = along_x.transpose(0, 2, 1)
    back_y = along_y.transpose(0, 2, 1) / PADDED**2
    spread = np.zeros((BAND, WIDE), np.float32)
    for b in range(BAND):
        for part in range(2):
            at = b // 4 * LANES + part * 64 + b % 4 * PIECE
            spread[b, at : at + PIECE] = 1.0
    first = np.stack(np_split(along_y), axis=1)
    second = np.stack([np.concatenate([h, h, l], axis=2) for h, l in (np_split(along_x), np_split(back_x))])
    third = np.stack(np_split(back_y))
    return first, second, third, spread.astype(ml_dtypes.bfloat16)


def dot(left, right):
    return jnp.dot(left, right, preferred_element_type=jnp.float32)


def dot3(left_high, left_low, right):
    high, low = split(right)
    if right.shape[1] > 256:
        return dot(left_high, jnp.concatenate([high, low, high], axis=0))
    return dot(left_high, high) + dot(left_high, low) + dot(left_low, high)


def turn(value, shift):
    shift %= LANES
    return value if shift == 0 else pltpu.roll(value, shift, 1)


def slot_of_lane(rows):
    return lax.broadcasted_iota(jnp.int32, (rows, LANES), 1) % 64 // PIECE


def gather_pieces(sources, slots):
    result = None
    for at, source in enumerate(sources):
        if source is None:
            continue
        moved = turn(source[0], PIECE * (at - source[1]))
        result = moved if result is None else jnp.where(slots == at, moved, result)
    return result


def transpose_pieces(tiles, slots):
    result = list(tiles)
    for step in (1, 2):
        low = slots // step % 2 == 0
        for at in (0, 1) if step == 2 else (0, 2):
            left, right = result[at], result[at + step]
            result[at] = jnp.where(low, left, turn(right, PIECE * step))
            result[at + step] = jnp.where(low, turn(left, -PIECE * step), right)
    return result


def times_minus_i(value):
    rows = value.shape[0]
    is_real = lax.broadcasted_iota(jnp.int32, (rows, LANES), 1) < 64
    parts = []
    for at in range(0, value.shape[1], LANES):
        turned = turn(value[:, at : at + LANES], 64)
        parts.append(jnp.where(is_real, turned, -turned))
    return jnp.concatenate(parts, axis=1)


def butterfly(a0, a1, a2, a3):
    even, odd = a0 + a2, a1 + a3
    apart, turned = a0 - a2, times_minus_i(a1 - a3)
    return even + odd, apart + turned, even - odd, apart - turned


def forward(high_ref_of, low_ref_of, residues):
    parts = []
    for r in range(4):
        data = jnp.concatenate([residues[r], times_minus_i(residues[r])], axis=0)
        parts.append(dot3(high_ref_of(r), low_ref_of(r), data))
    return butterfly(*parts)


def backward(high_ref_of, low_ref_of, quarters):
    sums = butterfly(*quarters)
    result = []
    for r, at in enumerate((0, 3, 2, 1)):
        both = dot3(high_ref_of(r), low_ref_of(r), sums[at])
        result.append(both[:80] - times_minus_i(both[80:]))
    return result


def gather_rows(sens_ref, rows_ref):
    for x in range(ROWS):
        for part in range(2):
            for j in range(COILS):
                row = (2 * x + part) * PIECE + 2 * j
                rows_ref[row : row + 2, :] = sens_ref[j, part, x]


def first_kernel(
    image_hbm, sens_hbm, table_hbm, out_ref,
    image_ref, sens_ref, table_ref, flat_ref, rows_ref, sems,
):
    copies = [
        pltpu.make_async_copy(sens_hbm, sens_ref, sems.at[0]),
        pltpu.make_async_copy(image_hbm, image_ref, sems.at[1]),
    ]
    for r in range(4):
        copies.append(pltpu.make_async_copy(table_hbm.at[r], table_ref.at[r], sems.at[2 + r]))
    for copy in copies:
        copy.start()
    copies[0].wait()
    gather_rows(sens_ref, rows_ref)
    copies[1].wait()
    real, imag = [], []
    for x in range(ROWS):
        sr = rows_ref[2 * x * PIECE : (2 * x + 1) * PIECE, :]
        si = rows_ref[(2 * x + 1) * PIECE : (2 * x + 2) * PIECE, :]
        ur = jnp.concatenate([image_ref[0, 0, x]] * COILS, axis=0)
        ui = jnp.concatenate([image_ref[0, 1, x]] * COILS, axis=0)
        real.append(sr * ur - si * ui)
        imag.append(sr * ui + si * ur)
    rest = [jnp.zeros((3 * PIECE, FULL), jnp.float32)]
    coil = jnp.concatenate(real[:4] + imag[:4] + real[4:] + rest + imag[4:] + rest, axis=0)
    coil = jnp.concatenate([coil, jnp.zeros((256, WIDE - FULL), jnp.float32)], axis=1).T
    flat_ref[0] = coil[:, :LANES]
    flat_ref[1] = coil[:, LANES:]
    residues = []
    for r in range(4):
        columns = [flat_ref[column, pl.ds(r, 80, stride=4), :] for column in range(2)]
        residues.append(jnp.concatenate(columns, axis=1))

    for r in range(4):
        copies[2 + r].wait()

    def table(r, level):
        return table_ref[r, level]

    bands = forward(lambda r: table(r, 0), lambda r: table(r, 1), residues)
    slots = slot_of_lane(16)
    for q in range(4):
        start = 16 * q * TILES

        def put(t, value):
            out_ref[pl.ds(start + t, 16, stride=TILES), :] = value

        near = [bands[q][b * 16 : (b + 1) * 16, :LANES] for b in range(BAND)]
        far = [bands[q][b * 16 : (b + 1) * 16, LANES:] for b in range(BAND)]
        for g in range(2):
            for x, value in enumerate(transpose_pieces(near[4 * g : 4 * g + 4], slots)):
                put(2 * x + g, value)
            put(8 + g, gather_pieces([(far[4 * g + i], 0) for i in range(4)], slots))
        for pair in range(2):
            pieces = [(near[8 + i], 2 * pair + x) for x in range(2) for i in range(2)]
            put(10 + pair, gather_pieces(pieces, slots))
        put(12, gather_pieces([(far[8], 0), (far[9], 0)], slots))


def weights(kern_ref, spread_ref):
    form = (((0,), (0,)), ((), ()))
    high, low = split(kern_ref[:, 0])
    return lax.dot_general(
        high, spread_ref[...], form, preferred_element_type=jnp.float32
    ) + lax.dot_general(low, spread_ref[...], form, preferred_element_type=jnp.float32)


def edge_kernel(image_ref, measured_ref, dual_ref, sens_ref, edge_ref, rim_ref, rows_ref):
    gather_rows(sens_ref, rows_ref)
    for at, count, source in ((0, 2, image_ref), (2, 2, measured_ref), (4, 6, dual_ref)):
        for channel in range(count):
            edge_ref[at + channel, 0] = source[0, channel, 0]
    for j in range(COILS):
        for part in range(2):
            edge_ref[10 + 2 * j + part, 0] = sens_ref[j, part, 0]
    for part in range(2):
        rim_ref[part, 0] = dual_ref[0, part, ROWS - 1]


def second_kernel(in_ref, kern_ref, spread_ref, table_ref, out_ref):
    weight = weights(kern_ref, spread_ref)

    def place(x, r, t):
        return pl.ds((r - x) % 4 * TILES + t, 16, stride=4 * TILES)

    residues = []
    for r in range(4):
        rows = []
        for x in range(ROWS):
            rest = turn(in_ref[place(x, r, 10 + x // 2), :], -2 * PIECE * (x % 2))
            whole = [in_ref[place(x, r, 2 * x), :], in_ref[place(x, r, 2 * x + 1), :]]
            rows.append(jnp.concatenate(whole + [rest], axis=1))
        residues.append(jnp.concatenate(rows, axis=0))
    spectrum = forward(lambda r: table_ref[0, r], lambda r: None, residues)
    weighted = [
        part * weight[q * QUARTER : (q + 1) * QUARTER, :] for q, part in enumerate(spectrum)
    ]
    result = backward(lambda r: table_ref[1, r], lambda r: None, weighted)
    lower = slot_of_lane(16) < 2
    for s in range(4):

        def put(t, value):
            out_ref[pl.ds(s * BACK_TILES + t, 16, stride=4 * BACK_TILES), :] = value

        rows = [result[(s + x) % 4][x * 16 : (x + 1) * 16] for x in range(ROWS)]
        following = result[(s + 1) % 4][:16]
        rows.append(pltpu.roll(following, 15, 0) if s == 3 else following)
        for x in range(ROWS + 1):
            for g in range(2):
                put(2 * x + g, rows[x][:, g * LANES : (g + 1) * LANES])
        for pair in range(3):
            left, right = rows[2 * pair][:, 2 * LANES :], rows[2 * pair + 1][:, 2 * LANES :]
            put(12 + pair, jnp.where(lower, left, turn(right, 2 * PIECE)))


def third_kernel(
    last_ref, in_ref, rows_ref, table_ref, image_ref, measured_ref, dual_ref, edge_ref, rim_ref,
    moved_ref, energy_ref, flat_ref, next_ref, plain_ref,
):
    slots = slot_of_lane(16)
    quarters = []
    for q in range(4):
        start = 16 * q * BACK_TILES
        tiles = [in_ref[pl.ds(start + t, 16, stride=BACK_TILES), :] for t in range(BACK_TILES)]
        near, far = [], []
        for g in range(2):
            near += transpose_pieces([tiles[2 * x + g] for x in range(4)], slots)
            far += [gather_pieces([(tiles[8 + g], i), (tiles[10 + g], i)], slots) for i in range(4)]
        for i in range(2):
            near.append(gather_pieces([(tiles[12 + x // 2], x % 2 * 2 + i) for x in range(4)], slots))
            far.append(gather_pieces([(tiles[14], i), (tiles[14], 2 + i)], slots))
        columns = [jnp.concatenate(near, axis=0), jnp.concatenate(far, axis=0)]
        quarters.append(jnp.concatenate(columns, axis=1))
    back = backward(lambda r: table_ref[0, r], lambda r: table_ref[1, r], quarters)
    flat_ref[:, FULL:, :] = jnp.zeros((2, WIDE - FULL, LANES), jnp.float32)
    for r in range(4):
        for column in range(2):
            flat_ref[column, pl.ds(r, 80, stride=4), :] = back[r][
                :, column * LANES : (column + 1) * LANES
            ]
    back = jnp.concatenate([flat_ref[0].T, flat_ref[1].T], axis=0)[:, :FULL]

    def over_coils(value):
        half = value[:8] + value[8:]
        quarter = half[:4] + half[4:]
        return quarter[:2] + quarter[2:]

    for part in range(2):
        plain_ref[12 + part, :2, :FULL] = rim_ref[part, 0]
        for j in range(COILS):
            row = part * PIECE + 2 * j
            next_ref[row : row + 2, :] = edge_ref[10 + 2 * j + part, 0]
    for source, at, count in ((image_ref, 0, 2), (measured_ref, 2, 2), (dual_ref, 4, 6)):
        for channel in range(count):
            for x in range(ROWS):
                plain_ref[at + channel, 2 * x : 2 * x + 2, :FULL] = source[0, channel, x]
            plain_ref[at + channel, 2 * ROWS : 2 * ROWS + 2, :FULL] = edge_ref[at + channel, 0]
    for x in range(ROWS + 1):
        if x < ROWS:
            at = 2 * x * PIECE
            sr, si = rows_ref[at : at + PIECE, :], rows_ref[at + PIECE : at + 2 * PIECE, :]
        else:
            sr, si = next_ref[:PIECE, :], next_ref[PIECE:, :]
        at = x // 4 * LANES + x % 4 * PIECE
        br, bi = back[at : at + PIECE], back[at + 64 : at + 64 + PIECE]
        plain_ref[10, 2 * x : 2 * x + 2, :FULL] = over_coils(sr * br + si * bi)
        plain_ref[11, 2 * x : 2 * x + 2, :FULL] = over_coils(sr * bi - si * br)

    row = lax.broadcasted_iota(jnp.int32, (16, WIDE), 0)
    lane = lax.broadcasted_iota(jnp.int32, (16, WIDE), 1)
    known = (lane < FULL) & (row < 2 * ROWS + 2)
    inner_y = lane < FULL - 1
    inner_z = row % 2 == 0
    inner_x = row < jnp.where(last_ref[0] > 0, 2 * ROWS - 2, 16)

    def field(at):
        return jnp.where(known, plain_ref[at], 0.0)

    moved = [None] * 6
    for part in range(2):
        own, across, through = field(4 + part), field(6 + part), field(8 + part)
        masked_x = jnp.where(inner_x, own, 0.0)
        masked_y = jnp.where(inner_y, across, 0.0)
        masked_z = jnp.where(inner_z, through, 0.0)
        before = jnp.where(row < 2, field(12 + part), pltpu.roll(masked_x, 2, 0))
        adjoint = (before - masked_x) + (pltpu.roll(masked_y, 1, 1) - masked_y)
        adjoint = adjoint + (pltpu.roll(masked_z, 1, 0) - masked_z)
        now = field(part)
        new = now - 0.2 * (field(10 + part) - field(2 + part) + adjoint)
        extra = 2.0 * new - now
        grad_x = jnp.where(inner_x, pltpu.roll(extra, 14, 0) - extra, 0.0)
        grad_y = jnp.where(inner_y, pltpu.roll(extra, WIDE - 1, 1) - extra, 0.0)
        grad_z = jnp.where(inner_z, pltpu.roll(extra, 15, 0) - extra, 0.0)
        moved[part] = own + 0.5 * grad_x
        moved[2 + part] = across + 0.5 * grad_y
        moved[4 + part] = through + 0.5 * grad_z
        moved_ref[6 + part] = new
    energy = sum(value * value for value in moved)
    for channel in range(6):
        moved_ref[channel] = moved[channel]
    for copy in range(energy_ref.shape[0]):
        for t in range(3):
            energy_ref[copy, 10 * t : 10 * t + 10, :] = energy[:10, t * LANES : (t + 1) * LANES]


def last_kernel(limit, energy_ref, moved_ref, new_ref, out_ref):
    energy = energy_ref[0]
    for at in range(1, energy_ref.shape[0]):
        energy = energy + energy_ref[at]
    scale = 1.0 / jnp.maximum(1.0, jnp.sqrt(energy) / limit)
    scale = jnp.concatenate([scale[10 * t : 10 * t + 10] for t in range(3)], axis=1)
    for channel in range(6):
        value = moved_ref[channel][:10] * scale
        for x in range(ROWS):
            out_ref[0, channel, x] = value[2 * x : 2 * x + 2, :FULL]
    for part in range(2):
        for x in range(ROWS):
            new_ref[0, part, x] = moved_ref[6 + part, 2 * x : 2 * x + 2, :FULL]


PARAMS = pltpu.CompilerParams(vmem_limit_bytes=32 * 2**20)


def exchange(value):
    tiles = value.shape[0] // SLABS
    blocks = value.reshape(SLABS, 1, tiles * LANES)
    return lax.all_to_all(blocks, "slab", 0, 0, tiled=True).reshape(SLABS * tiles, LANES)


def shifted(value, axis, by):
    count = lax.axis_size(axis)
    pairs = [(i, i + by) for i in range(count) if 0 <= i + by < count]
    return lax.ppermute(value, axis, pairs)


def local(image, dual, adjoint_data, sens, kern):
    image, dual, adjoint_data, sens = (
        jnp.swapaxes(value, 2, 3) for value in (image, dual, adjoint_data, sens)
    )
    first, second, third, spread = tables()
    contrasts = lax.axis_size("con")
    whole = pl.BlockSpec(memory_space=pltpu.HBM)
    bands = pl.pallas_call(
        first_kernel,
        in_specs=[whole] * 3,
        out_shape=jax.ShapeDtypeStruct((SLABS * TILES, LANES), jnp.float32),
        scratch_shapes=[
            pltpu.VMEM(image.shape, jnp.float32),
            pltpu.VMEM(sens.shape, jnp.float32),
            pltpu.VMEM(first.shape, jnp.bfloat16),
            pltpu.VMEM((2, WIDE, LANES), jnp.float32),
            pltpu.VMEM((2 * ROWS * PIECE, FULL), jnp.float32),
            pltpu.SemaphoreType.DMA((6,)),
        ],
        compiler_params=pltpu.CompilerParams(vmem_limit_bytes=53 * 2**20),
        name="first",
    )(image, sens, first)
    returned = pl.pallas_call(
        second_kernel,
        out_shape=jax.ShapeDtypeStruct((SLABS * BACK_TILES, LANES), jnp.float32),
        compiler_params=PARAMS,
        name="second",
    )(exchange(bands), kern.reshape(BAND, 1, PADDED), spread, second)
    *late, returned = lax.optimization_barrier((image, adjoint_data, dual, sens, returned))
    edge, rim, sens_rows = pl.pallas_call(
        edge_kernel,
        out_shape=(
            jax.ShapeDtypeStruct((10 + 2 * COILS, 1, PLANES, FULL), jnp.float32),
            jax.ShapeDtypeStruct((2, 1, PLANES, FULL), jnp.float32),
            jax.ShapeDtypeStruct((2 * ROWS * PIECE, FULL), jnp.float32),
        ),
        compiler_params=PARAMS,
        name="edge",
    )(*late)
    edge = shifted(edge, "slab", -1)
    rim = shifted(rim, "slab", 1)
    is_last = (lax.axis_index("slab") == SLABS - 1).astype(jnp.int32).reshape(1)
    moved, energy = pl.pallas_call(
        third_kernel,
        in_specs=[pl.BlockSpec(memory_space=pltpu.SMEM)]
        + [pl.BlockSpec(memory_space=pltpu.VMEM)] * 8,
        out_shape=(
            jax.ShapeDtypeStruct((8, 16, WIDE), jnp.float32),
            jax.ShapeDtypeStruct((contrasts, 30, LANES), jnp.float32),
        ),
        scratch_shapes=[
            pltpu.VMEM((2, WIDE, LANES), jnp.float32),
            pltpu.VMEM((2 * PIECE, FULL), jnp.float32),
            pltpu.VMEM((14, 16, WIDE), jnp.float32),
        ],
        compiler_params=PARAMS,
        name="third",
    )(is_last, exchange(returned), sens_rows, third, image, adjoint_data, dual, edge, rim)
    new_image, new_dual = pl.pallas_call(
        functools.partial(last_kernel, 0.9 * math.sqrt(6.0 * contrasts)),
        out_shape=(
            jax.ShapeDtypeStruct(image.shape, jnp.float32),
            jax.ShapeDtypeStruct(dual.shape, jnp.float32),
        ),
        compiler_params=PARAMS,
        name="last",
    )(lax.all_to_all(energy, "con", 0, 0, tiled=True), moved)
    return jnp.swapaxes(new_image, 2, 3), jnp.swapaxes(new_dual, 2, 3)


def solution(mesh):
    return jax.shard_map(
        local,
        mesh=mesh,
        in_specs=(
            P("con", None, None, "slab", None),
            P("con", None, None, "slab", None),
            P("con", None, None, "slab", None),
            P(None, None, None, "slab", None),
            P("con", "slab", None),
        ),
        out_specs=(P("con", None, None, "slab", None), P("con", None, None, "slab", None)),
        check_vma=False,
    )
```

```python
import functools
import math

import jax
import jax.numpy as jnp
import ml_dtypes
import numpy as np
from jax import lax
from jax.experimental import pallas as pl
from jax.experimental.pallas import tpu as pltpu
from jax.sharding import PartitionSpec as P

FULL = 320
PADDED = 640
QUARTER = 160
SLABS = 64
ROWS = 5
BAND = 10
COILS = 8
PLANES = 2
PIECE = PLANES * COILS
TILES = 13
BACK_TILES = 15
LANES = 128
WIDE = 384


def tile_of(x, b, rows):
    if b < 8:
        return 2 * x + b // 4, b % 4
    return 2 * rows + x // 2, (x % 2) * 2 + b - 8


def split(value):
    high = value.astype(jnp.bfloat16)
    return high, (value - high.astype(jnp.float32)).astype(jnp.bfloat16)


def np_split(value):
    high = value.astype(np.float32).astype(ml_dtypes.bfloat16)
    low = (value - high.astype(np.float64)).astype(np.float32).astype(ml_dtypes.bfloat16)
    return high, low


@functools.cache
def tables():
    low = np.arange(QUARTER)
    by_band = (np.arange(BAND)[:, None] + BAND * np.arange(16)[None, :]).reshape(-1)
    points_y = [4 * np.arange(80) + r for r in range(4)]
    points_x = []
    for r in range(4):
        order = [5 * (4 * u + (r - x) % 4) + x for x in range(ROWS) for u in range(16)]
        points_x.append(np.array(order))

    def stack(points, k):
        result = []
        for point in points:
            angle = 2 * np.pi * (k[:, None] * point[None, :] % PADDED) / PADDED
            result.append(np.concatenate([np.cos(angle), np.sin(angle)], axis=1))
        return np.stack(result)

    along_y = stack(points_y, by_band)
    along_x = stack(points_x, low)
    back_x = along_x.transpose(0, 2, 1)
    back_y = along_y.transpose(0, 2, 1) / PADDED**2
    spread = np.zeros((BAND, WIDE), np.float32)
    for b in range(BAND):
        for part in range(2):
            at = b // 4 * LANES + part * 64 + b % 4 * PIECE
            spread[b, at : at + PIECE] = 1.0
    first = np.stack(np_split(along_y), axis=1)
    second = np.stack([np.concatenate([h, h, l], axis=2) for h, l in (np_split(along_x), np_split(back_x))])
    third = np.stack(np_split(back_y))
    return first, second, third, spread.astype(ml_dtypes.bfloat16)


def dot(left, right):
    return jnp.dot(left, right, preferred_element_type=jnp.float32)


def dot3(left_high, left_low, right):
    high, low = split(right)
    if right.shape[1] > 256:
        return dot(left_high, jnp.concatenate([high, low, high], axis=0))
    return dot(left_high, high) + dot(left_high, low) + dot(left_low, high)


def turn(value, shift):
    shift %= LANES
    return value if shift == 0 else pltpu.roll(value, shift, 1)


def slot_of_lane(rows):
    return lax.broadcasted_iota(jnp.int32, (rows, LANES), 1) % 64 // PIECE


def gather_pieces(sources, slots):
    result = None
    for at, source in enumerate(sources):
        if source is None:
            continue
        moved = turn(source[0], PIECE * (at - source[1]))
        result = moved if result is None else jnp.where(slots == at, moved, result)
    return result


def transpose_pieces(tiles, slots):
    result = list(tiles)
    for step in (1, 2):
        low = slots // step % 2 == 0
        for at in (0, 1) if step == 2 else (0, 2):
            left, right = result[at], result[at + step]
            result[at] = jnp.where(low, left, turn(right, PIECE * step))
            result[at + step] = jnp.where(low, turn(left, -PIECE * step), right)
    return result


def times_minus_i(value):
    rows = value.shape[0]
    is_real = lax.broadcasted_iota(jnp.int32, (rows, LANES), 1) < 64
    parts = []
    for at in range(0, value.shape[1], LANES):
        turned = turn(value[:, at : at + LANES], 64)
        parts.append(jnp.where(is_real, turned, -turned))
    return jnp.concatenate(parts, axis=1)


def butterfly(a0, a1, a2, a3):
    even, odd = a0 + a2, a1 + a3
    apart, turned = a0 - a2, times_minus_i(a1 - a3)
    return even + odd, apart + turned, even - odd, apart - turned


def forward(high_ref_of, low_ref_of, residues):
    parts = []
    for r in range(4):
        data = jnp.concatenate([residues[r], times_minus_i(residues[r])], axis=0)
        parts.append(dot3(high_ref_of(r), low_ref_of(r), data))
    return butterfly(*parts)


def backward(high_ref_of, low_ref_of, quarters):
    sums = butterfly(*quarters)
    result = []
    for r, at in enumerate((0, 3, 2, 1)):
        both = dot3(high_ref_of(r), low_ref_of(r), sums[at])
        result.append(both[:80] - times_minus_i(both[80:]))
    return result


def gather_rows(sens_ref, rows_ref):
    for x in range(ROWS):
        for part in range(2):
            for j in range(COILS):
                row = (2 * x + part) * PIECE + 2 * j
                rows_ref[row : row + 2, :] = sens_ref[j, part, x]


def first_kernel(
    image_hbm, sens_hbm, table_hbm, out_ref,
    image_ref, sens_ref, table_ref, flat_ref, rows_ref, sems,
):
    copies = [
        pltpu.make_async_copy(sens_hbm, sens_ref, sems.at[0]),
        pltpu.make_async_copy(image_hbm, image_ref, sems.at[1]),
    ]
    for r in range(4):
        copies.append(pltpu.make_async_copy(table_hbm.at[r], table_ref.at[r], sems.at[2 + r]))
    for copy in copies:
        copy.start()
    copies[0].wait()
    gather_rows(sens_ref, rows_ref)
    copies[1].wait()
    real, imag = [], []
    for x in range(ROWS):
        sr = rows_ref[2 * x * PIECE : (2 * x + 1) * PIECE, :]
        si = rows_ref[(2 * x + 1) * PIECE : (2 * x + 2) * PIECE, :]
        ur = jnp.concatenate([image_ref[0, 0, x]] * COILS, axis=0)
        ui = jnp.concatenate([image_ref[0, 1, x]] * COILS, axis=0)
        real.append(sr * ur - si * ui)
        imag.append(sr * ui + si * ur)
    rest = [jnp.zeros((3 * PIECE, FULL), jnp.float32)]
    coil = jnp.concatenate(real[:4] + imag[:4] + real[4:] + rest + imag[4:] + rest, axis=0)
    coil = jnp.concatenate([coil, jnp.zeros((256, WIDE - FULL), jnp.float32)], axis=1).T
    flat_ref[0] = coil[:, :LANES]
    flat_ref[1] = coil[:, LANES:]
    residues = []
    for r in range(4):
        columns = [flat_ref[column, pl.ds(r, 80, stride=4), :] for column in range(2)]
        residues.append(jnp.concatenate(columns, axis=1))

    for r in range(4):
        copies[2 + r].wait()

    def table(r, level):
        return table_ref[r, level]

    bands = forward(lambda r: table(r, 0), lambda r: table(r, 1), residues)
    slots = slot_of_lane(16)
    for q in range(4):
        start = 16 * q * TILES

        def put(t, value):
            out_ref[pl.ds(start + t, 16, stride=TILES), :] = value

        near = [bands[q][b * 16 : (b + 1) * 16, :LANES] for b in range(BAND)]
        far = [bands[q][b * 16 : (b + 1) * 16, LANES:] for b in range(BAND)]
        for g in range(2):
            for x, value in enumerate(transpose_pieces(near[4 * g : 4 * g + 4], slots)):
                put(2 * x + g, value)
            put(8 + g, gather_pieces([(far[4 * g + i], 0) for i in range(4)], slots))
        for pair in range(2):
            pieces = [(near[8 + i], 2 * pair + x) for x in range(2) for i in range(2)]
            put(10 + pair, gather_pieces(pieces, slots))
        put(12, gather_pieces([(far[8], 0), (far[9], 0)], slots))


def weight_kernel(kern_ref, spread_ref, out_ref):
    form = (((0,), (0,)), ((), ()))
    high, low = split(kern_ref[0])
    out_ref[...] = lax.dot_general(
        high, spread_ref[...], form, preferred_element_type=jnp.float32
    ) + lax.dot_general(low, spread_ref[...], form, preferred_element_type=jnp.float32)


def edge_kernel(image_ref, measured_ref, dual_ref, sens_ref, edge_ref, rim_ref, rows_ref):
    gather_rows(sens_ref, rows_ref)
    for at, count, source in ((0, 2, image_ref), (2, 2, measured_ref), (4, 6, dual_ref)):
        for channel in range(count):
            edge_ref[at + channel, 0] = source[0, channel, 0]
    for j in range(COILS):
        for part in range(2):
            edge_ref[10 + 2 * j + part, 0] = sens_ref[j, part, 0]
    for part in range(2):
        rim_ref[part, 0] = dual_ref[0, part, ROWS - 1]


def second_kernel(in_ref, weight_ref, table_ref, out_ref):
    def place(x, r, t):
        return pl.ds((r - x) % 4 * TILES + t, 16, stride=4 * TILES)

    residues = []
    for r in range(4):
        rows = []
        for x in range(ROWS):
            rest = turn(in_ref[place(x, r, 10 + x // 2), :], -2 * PIECE * (x % 2))
            whole = [in_ref[place(x, r, 2 * x), :], in_ref[place(x, r, 2 * x + 1), :]]
            rows.append(jnp.concatenate(whole + [rest], axis=1))
        residues.append(jnp.concatenate(rows, axis=0))
    spectrum = forward(lambda r: table_ref[0, r], lambda r: None, residues)
    weighted = [
        part * weight_ref[q * QUARTER : (q + 1) * QUARTER, :] for q, part in enumerate(spectrum)
    ]
    result = backward(lambda r: table_ref[1, r], lambda r: None, weighted)
    lower = slot_of_lane(16) < 2
    for s in range(4):

        def put(t, value):
            out_ref[pl.ds(s * BACK_TILES + t, 16, stride=4 * BACK_TILES), :] = value

        rows = [result[(s + x) % 4][x * 16 : (x + 1) * 16] for x in range(ROWS)]
        following = result[(s + 1) % 4][:16]
        rows.append(pltpu.roll(following, 15, 0) if s == 3 else following)
        for x in range(ROWS + 1):
            for g in range(2):
                put(2 * x + g, rows[x][:, g * LANES : (g + 1) * LANES])
        for pair in range(3):
            left, right = rows[2 * pair][:, 2 * LANES :], rows[2 * pair + 1][:, 2 * LANES :]
            put(12 + pair, jnp.where(lower, left, turn(right, 2 * PIECE)))


def third_kernel(
    last_ref, in_ref, rows_ref, table_ref, image_ref, measured_ref, dual_ref, edge_ref, rim_ref,
    moved_ref, energy_ref, flat_ref, next_ref, plain_ref,
):
    slots = slot_of_lane(16)
    quarters = []
    for q in range(4):
        start = 16 * q * BACK_TILES
        tiles = [in_ref[pl.ds(start + t, 16, stride=BACK_TILES), :] for t in range(BACK_TILES)]
        near, far = [], []
        for g in range(2):
            near += transpose_pieces([tiles[2 * x + g] for x in range(4)], slots)
            far += [gather_pieces([(tiles[8 + g], i), (tiles[10 + g], i)], slots) for i in range(4)]
        for i in range(2):
            near.append(gather_pieces([(tiles[12 + x // 2], x % 2 * 2 + i) for x in range(4)], slots))
            far.append(gather_pieces([(tiles[14], i), (tiles[14], 2 + i)], slots))
        columns = [jnp.concatenate(near, axis=0), jnp.concatenate(far, axis=0)]
        quarters.append(jnp.concatenate(columns, axis=1))
    back = backward(lambda r: table_ref[0, r], lambda r: table_ref[1, r], quarters)
    flat_ref[:, FULL:, :] = jnp.zeros((2, WIDE - FULL, LANES), jnp.float32)
    for r in range(4):
        for column in range(2):
            flat_ref[column, pl.ds(r, 80, stride=4), :] = back[r][
                :, column * LANES : (column + 1) * LANES
            ]
    back = jnp.concatenate([flat_ref[0].T, flat_ref[1].T], axis=0)[:, :FULL]

    def over_coils(value):
        half = value[:8] + value[8:]
        quarter = half[:4] + half[4:]
        return quarter[:2] + quarter[2:]

    for part in range(2):
        plain_ref[12 + part, :2, :FULL] = rim_ref[part, 0]
        for j in range(COILS):
            row = part * PIECE + 2 * j
            next_ref[row : row + 2, :] = edge_ref[10 + 2 * j + part, 0]
    for source, at, count in ((image_ref, 0, 2), (measured_ref, 2, 2), (dual_ref, 4, 6)):
        for channel in range(count):
            for x in range(ROWS):
                plain_ref[at + channel, 2 * x : 2 * x + 2, :FULL] = source[0, channel, x]
            plain_ref[at + channel, 2 * ROWS : 2 * ROWS + 2, :FULL] = edge_ref[at + channel, 0]
    for x in range(ROWS + 1):
        if x < ROWS:
            at = 2 * x * PIECE
            sr, si = rows_ref[at : at + PIECE, :], rows_ref[at + PIECE : at + 2 * PIECE, :]
        else:
            sr, si = next_ref[:PIECE, :], next_ref[PIECE:, :]
        at = x // 4 * LANES + x % 4 * PIECE
        br, bi = back[at : at + PIECE], back[at + 64 : at + 64 + PIECE]
        plain_ref[10, 2 * x : 2 * x + 2, :FULL] = over_coils(sr * br + si * bi)
        plain_ref[11, 2 * x : 2 * x + 2, :FULL] = over_coils(sr * bi - si * br)

    row = lax.broadcasted_iota(jnp.int32, (16, WIDE), 0)
    lane = lax.broadcasted_iota(jnp.int32, (16, WIDE), 1)
    known = (lane < FULL) & (row < 2 * ROWS + 2)
    inner_y = lane < FULL - 1
    inner_z = row % 2 == 0
    inner_x = row < jnp.where(last_ref[0] > 0, 2 * ROWS - 2, 16)

    def field(at):
        return jnp.where(known, plain_ref[at], 0.0)

    moved = [None] * 6
    for part in range(2):
        own, across, through = field(4 + part), field(6 + part), field(8 + part)
        masked_x = jnp.where(inner_x, own, 0.0)
        masked_y = jnp.where(inner_y, across, 0.0)
        masked_z = jnp.where(inner_z, through, 0.0)
        before = jnp.where(row < 2, field(12 + part), pltpu.roll(masked_x, 2, 0))
        adjoint = (before - masked_x) + (pltpu.roll(masked_y, 1, 1) - masked_y)
        adjoint = adjoint + (pltpu.roll(masked_z, 1, 0) - masked_z)
        now = field(part)
        new = now - 0.2 * (field(10 + part) - field(2 + part) + adjoint)
        extra = 2.0 * new - now
        grad_x = jnp.where(inner_x, pltpu.roll(extra, 14, 0) - extra, 0.0)
        grad_y = jnp.where(inner_y, pltpu.roll(extra, WIDE - 1, 1) - extra, 0.0)
        grad_z = jnp.where(inner_z, pltpu.roll(extra, 15, 0) - extra, 0.0)
        moved[part] = own + 0.5 * grad_x
        moved[2 + part] = across + 0.5 * grad_y
        moved[4 + part] = through + 0.5 * grad_z
        moved_ref[6 + part] = new
    energy = sum(value * value for value in moved)
    for channel in range(6):
        moved_ref[channel] = moved[channel]
    for copy in range(energy_ref.shape[0]):
        for t in range(3):
            energy_ref[copy, 10 * t : 10 * t + 10, :] = energy[:10, t * LANES : (t + 1) * LANES]


def last_kernel(limit, energy_ref, moved_ref, new_ref, out_ref):
    energy = energy_ref[0]
    for at in range(1, energy_ref.shape[0]):
        energy = energy + energy_ref[at]
    scale = 1.0 / jnp.maximum(1.0, jnp.sqrt(energy) / limit)
    scale = jnp.concatenate([scale[10 * t : 10 * t + 10] for t in range(3)], axis=1)
    for channel in range(6):
        value = moved_ref[channel][:10] * scale
        for x in range(ROWS):
            out_ref[0, channel, x] = value[2 * x : 2 * x + 2, :FULL]
    for part in range(2):
        for x in range(ROWS):
            new_ref[0, part, x] = moved_ref[6 + part, 2 * x : 2 * x + 2, :FULL]


PARAMS = pltpu.CompilerParams(vmem_limit_bytes=32 * 2**20)


def exchange(value):
    tiles = value.shape[0] // SLABS
    blocks = value.reshape(SLABS, 1, tiles * LANES)
    return lax.all_to_all(blocks, "slab", 0, 0, tiled=True).reshape(SLABS * tiles, LANES)


def shifted(value, axis, by):
    count = lax.axis_size(axis)
    pairs = [(i, i + by) for i in range(count) if 0 <= i + by < count]
    return lax.ppermute(value, axis, pairs)


def local(image, dual, adjoint_data, sens, kern):
    image, dual, adjoint_data, sens = (
        jnp.swapaxes(value, 2, 3) for value in (image, dual, adjoint_data, sens)
    )
    first, second, third, spread = tables()
    contrasts = lax.axis_size("con")
    weight = pl.pallas_call(
        weight_kernel,
        out_shape=jax.ShapeDtypeStruct((PADDED, WIDE), jnp.float32),
        compiler_params=PARAMS,
        name="weights",
    )(kern, spread)
    whole = pl.BlockSpec(memory_space=pltpu.HBM)
    bands = pl.pallas_call(
        first_kernel,
        in_specs=[whole] * 3,
        out_shape=jax.ShapeDtypeStruct((SLABS * TILES, LANES), jnp.float32),
        scratch_shapes=[
            pltpu.VMEM(image.shape, jnp.float32),
            pltpu.VMEM(sens.shape, jnp.float32),
            pltpu.VMEM(first.shape, jnp.bfloat16),
            pltpu.VMEM((2, WIDE, LANES), jnp.float32),
            pltpu.VMEM((2 * ROWS * PIECE, FULL), jnp.float32),
            pltpu.SemaphoreType.DMA((6,)),
        ],
        compiler_params=PARAMS,
        name="first",
    )(*(pltpu.with_memory_space_constraint(v, pltpu.HBM) for v in (image, sens, first)))
    edge, rim, sens_rows = pl.pallas_call(
        edge_kernel,
        out_shape=(
            jax.ShapeDtypeStruct((10 + 2 * COILS, 1, PLANES, FULL), jnp.float32),
            jax.ShapeDtypeStruct((2, 1, PLANES, FULL), jnp.float32),
            jax.ShapeDtypeStruct((2 * ROWS * PIECE, FULL), jnp.float32),
        ),
        compiler_params=PARAMS,
        name="edge",
    )(image, adjoint_data, dual, sens)
    edge = shifted(edge, "slab", -1)
    rim = shifted(rim, "slab", 1)
    is_last = (lax.axis_index("slab") == SLABS - 1).astype(jnp.int32).reshape(1)
    bands, edge, rim, is_last, sens_rows = lax.optimization_barrier(
        (exchange(bands), edge, rim, is_last, sens_rows)
    )
    returned = pl.pallas_call(
        second_kernel,
        out_shape=jax.ShapeDtypeStruct((SLABS * BACK_TILES, LANES), jnp.float32),
        compiler_params=PARAMS,
        name="second",
    )(bands, weight, second)
    moved, energy = pl.pallas_call(
        third_kernel,
        in_specs=[pl.BlockSpec(memory_space=pltpu.SMEM)]
        + [pl.BlockSpec(memory_space=pltpu.VMEM)] * 8,
        out_shape=(
            jax.ShapeDtypeStruct((8, 16, WIDE), jnp.float32),
            jax.ShapeDtypeStruct((contrasts, 30, LANES), jnp.float32),
        ),
        scratch_shapes=[
            pltpu.VMEM((2, WIDE, LANES), jnp.float32),
            pltpu.VMEM((2 * PIECE, FULL), jnp.float32),
            pltpu.VMEM((14, 16, WIDE), jnp.float32),
        ],
        compiler_params=PARAMS,
        name="third",
    )(is_last, exchange(returned), sens_rows, third, image, adjoint_data, dual, edge, rim)
    new_image, new_dual = pl.pallas_call(
        functools.partial(last_kernel, 0.9 * math.sqrt(6.0 * contrasts)),
        out_shape=(
            jax.ShapeDtypeStruct(image.shape, jnp.float32),
            jax.ShapeDtypeStruct(dual.shape, jnp.float32),
        ),
        compiler_params=PARAMS,
        name="last",
    )(lax.all_to_all(energy, "con", 0, 0, tiled=True), moved)
    return jnp.swapaxes(new_image, 2, 3), jnp.swapaxes(new_dual, 2, 3)


def solution(mesh):
    return jax.shard_map(
        local,
        mesh=mesh,
        in_specs=(
            P("con", None, None, "slab", None),
            P("con", None, None, "slab", None),
            P("con", None, None, "slab", None),
            P(None, None, None, "slab", None),
            P("con", "slab", None),
        ),
        out_specs=(P("con", None, None, "slab", None), P("con", None, None, "slab", None)),
        check_vma=False,
    )
```

```python
import functools
import math

import jax
import jax.numpy as jnp
import ml_dtypes
import numpy as np
from jax import lax
from jax.experimental import pallas as pl
from jax.experimental.pallas import tpu as pltpu
from jax.sharding import PartitionSpec as P

FULL = 320
PADDED = 640
QUARTER = 160
SLABS = 64
ROWS = 5
BAND = 10
COILS = 8
PLANES = 2
PIECE = PLANES * COILS
TILES = 13
BACK_TILES = 15
LANES = 128
WIDE = 384


def tile_of(x, b, rows):
    if b < 8:
        return 2 * x + b // 4, b % 4
    return 2 * rows + x // 2, (x % 2) * 2 + b - 8


def split(value):
    high = value.astype(jnp.bfloat16)
    return high, (value - high.astype(jnp.float32)).astype(jnp.bfloat16)


def np_split(value):
    high = value.astype(np.float32).astype(ml_dtypes.bfloat16)
    low = (value - high.astype(np.float64)).astype(np.float32).astype(ml_dtypes.bfloat16)
    return high, low


def stack_depth(value):
    high, low = np_split(value)
    return np.concatenate([high, high, low], axis=-1)


@functools.cache
def tables():
    low = np.arange(QUARTER)
    by_band = (np.arange(BAND)[:, None] + BAND * np.arange(16)[None, :]).reshape(-1)
    points_y = [4 * np.arange(80) + r for r in range(4)]
    points_x = []
    for r in range(4):
        order = [5 * (4 * u + (r - x) % 4) + x for x in range(ROWS) for u in range(16)]
        points_x.append(np.array(order))

    def stack(points, k):
        result = []
        for point in points:
            angle = 2 * np.pi * (k[:, None] * point[None, :] % PADDED) / PADDED
            result.append(np.concatenate([np.cos(angle), np.sin(angle)], axis=1))
        return np.stack(result)

    along_y = stack(points_y, by_band)
    along_x = stack(points_x, low)
    back_x = along_x.transpose(0, 2, 1)
    back_y = along_y.transpose(0, 2, 1) / PADDED**2
    spread = np.zeros((BAND, WIDE), np.float32)
    for b in range(BAND):
        for part in range(2):
            at = b // 4 * LANES + part * 64 + b % 4 * PIECE
            spread[b, at : at + PIECE] = 1.0
    first, back_y = stack_depth(along_y), stack_depth(back_y)
    second = np.stack([stack_depth(along_x), stack_depth(back_x)])
    return first, second, back_y, spread.astype(ml_dtypes.bfloat16)


def dot(left, right):
    return jnp.dot(left, right, preferred_element_type=jnp.float32)


def dot3(left, right):
    high, low = split(right)
    return dot(left, jnp.concatenate([high, low, high], axis=0))


def turn(value, shift):
    shift %= LANES
    return value if shift == 0 else pltpu.roll(value, shift, 1)


def slot_of_lane(rows):
    return lax.broadcasted_iota(jnp.int32, (rows, LANES), 1) % 64 // PIECE


def gather_pieces(sources, slots):
    result = None
    for at, source in enumerate(sources):
        if source is None:
            continue
        moved = turn(source[0], PIECE * (at - source[1]))
        result = moved if result is None else jnp.where(slots == at, moved, result)
    return result


def trade(left, right, step, slots):
    low = slots // step % 2 == 0
    shift = PIECE * step
    return jnp.where(low, left, turn(right, shift)), jnp.where(low, turn(left, -shift), right)


def transpose_pieces(tiles, slots):
    a0, a1 = trade(tiles[0], tiles[1], 1, slots)
    a2, a3 = trade(tiles[2], tiles[3], 1, slots)
    b0, b2 = trade(a0, a2, 2, slots)
    b1, b3 = trade(a1, a3, 2, slots)
    return b0, b1, b2, b3


def times_minus_i(value):
    rows = value.shape[0]
    is_real = lax.broadcasted_iota(jnp.int32, (rows, LANES), 1) < 64
    parts = []
    for at in range(0, value.shape[1], LANES):
        turned = turn(value[:, at : at + LANES], 64)
        parts.append(jnp.where(is_real, turned, -turned))
    return jnp.concatenate(parts, axis=1)


def butterfly(a0, a1, a2, a3):
    even, odd = a0 + a2, a1 + a3
    apart, turned = a0 - a2, times_minus_i(a1 - a3)
    return even + odd, apart + turned, even - odd, apart - turned


def forward(table, residues):
    parts = []
    for r in range(4):
        data = jnp.concatenate([residues[r], times_minus_i(residues[r])], axis=0)
        parts.append(dot3(table[r], data))
    return butterfly(*parts)


def backward(table, quarters):
    sums = butterfly(*quarters)
    result = []
    for r, at in enumerate((0, 3, 2, 1)):
        both = dot3(table[r], sums[at])
        result.append(both[:80] - times_minus_i(both[80:]))
    return result


def gather_rows(sens_ref, rows_ref):
    for x in range(ROWS):
        for part in range(2):
            for j in range(COILS):
                row = (2 * x + part) * PIECE + 2 * j
                rows_ref[row : row + 2, :] = sens_ref[j, part, x]


def first_kernel(
    image_hbm, sens_hbm, table_hbm, out_ref,
    image_ref, sens_ref, table_ref, flat_ref, rows_ref, sems,
):
    copies = [
        pltpu.make_async_copy(sens_hbm, sens_ref, sems.at[0]),
        pltpu.make_async_copy(image_hbm, image_ref, sems.at[1]),
    ]
    for r in range(4):
        copies.append(pltpu.make_async_copy(table_hbm.at[r], table_ref.at[r], sems.at[2 + r]))
    for copy in copies:
        copy.start()
    copies[0].wait()
    gather_rows(sens_ref, rows_ref)
    copies[1].wait()
    real, imag = [], []
    for x in range(ROWS):
        sr = rows_ref[2 * x * PIECE : (2 * x + 1) * PIECE, :]
        si = rows_ref[(2 * x + 1) * PIECE : (2 * x + 2) * PIECE, :]
        ur = jnp.concatenate([image_ref[0, 0, x]] * COILS, axis=0)
        ui = jnp.concatenate([image_ref[0, 1, x]] * COILS, axis=0)
        real.append(sr * ur - si * ui)
        imag.append(sr * ui + si * ur)
    rest = [jnp.zeros((3 * PIECE, FULL), jnp.float32)]
    coil = jnp.concatenate(real[:4] + imag[:4] + real[4:] + rest + imag[4:] + rest, axis=0)
    coil = jnp.concatenate([coil, jnp.zeros((256, WIDE - FULL), jnp.float32)], axis=1).T
    flat_ref[0] = coil[:, :LANES]
    flat_ref[1] = coil[:, LANES:]
    residues = []
    for r in range(4):
        columns = [flat_ref[column, pl.ds(r, 80, stride=4), :] for column in range(2)]
        residues.append(jnp.concatenate(columns, axis=1))

    for r in range(4):
        copies[2 + r].wait()
    bands = forward(table_ref, residues)
    slots = slot_of_lane(16)
    for q in range(4):
        start = 16 * q * TILES

        def put(t, value):
            out_ref[pl.ds(start + t, 16, stride=TILES), :] = value

        near = [bands[q][b * 16 : (b + 1) * 16, :LANES] for b in range(BAND)]
        far = [bands[q][b * 16 : (b + 1) * 16, LANES:] for b in range(BAND)]
        for g in range(2):
            for x, value in enumerate(transpose_pieces(near[4 * g : 4 * g + 4], slots)):
                put(2 * x + g, value)
            put(8 + g, gather_pieces([(far[4 * g + i], 0) for i in range(4)], slots))
        for pair, value in enumerate(trade(*trade(near[8], near[9], 1, slots), 2, slots)):
            put(10 + pair, value)
        put(12, gather_pieces([(far[8], 0), (far[9], 0)], slots))


def weight_kernel(kern_ref, spread_ref, out_ref):
    form = (((0,), (0,)), ((), ()))
    high, low = split(kern_ref[0])
    out_ref[...] = lax.dot_general(
        high, spread_ref[...], form, preferred_element_type=jnp.float32
    ) + lax.dot_general(low, spread_ref[...], form, preferred_element_type=jnp.float32)


def edge_kernel(image_ref, measured_ref, dual_ref, sens_ref, edge_ref, rim_ref, rows_ref):
    gather_rows(sens_ref, rows_ref)
    for at, count, source in ((0, 2, image_ref), (2, 2, measured_ref), (4, 6, dual_ref)):
        for channel in range(count):
            edge_ref[at + channel, 0] = source[0, channel, 0]
    for j in range(COILS):
        for part in range(2):
            edge_ref[10 + 2 * j + part, 0] = sens_ref[j, part, 0]
    for part in range(2):
        rim_ref[part, 0] = dual_ref[0, part, ROWS - 1]


def second_kernel(in_ref, weight_ref, table_ref, out_ref):
    def place(x, r, t):
        return pl.ds((r - x) % 4 * TILES + t, 16, stride=4 * TILES)

    residues = []
    for r in range(4):
        rows = []
        for x in range(ROWS):
            rest = turn(in_ref[place(x, r, 10 + x // 2), :], -2 * PIECE * (x % 2))
            whole = [in_ref[place(x, r, 2 * x), :], in_ref[place(x, r, 2 * x + 1), :]]
            rows.append(jnp.concatenate(whole + [rest], axis=1))
        residues.append(jnp.concatenate(rows, axis=0))
    spectrum = forward(table_ref.at[0], residues)
    weighted = [
        part * weight_ref[q * QUARTER : (q + 1) * QUARTER, :] for q, part in enumerate(spectrum)
    ]
    result = backward(table_ref.at[1], weighted)
    lower = slot_of_lane(16) < 2
    for s in range(4):

        def put(t, value):
            out_ref[pl.ds(s * BACK_TILES + t, 16, stride=4 * BACK_TILES), :] = value

        rows = [result[(s + x) % 4][x * 16 : (x + 1) * 16] for x in range(ROWS)]
        following = result[(s + 1) % 4][:16]
        rows.append(pltpu.roll(following, 15, 0) if s == 3 else following)
        for x in range(ROWS + 1):
            for g in range(2):
                put(2 * x + g, rows[x][:, g * LANES : (g + 1) * LANES])
        for pair in range(3):
            left, right = rows[2 * pair][:, 2 * LANES :], rows[2 * pair + 1][:, 2 * LANES :]
            put(12 + pair, jnp.where(lower, left, turn(right, 2 * PIECE)))


def third_kernel(
    last_ref, in_ref, rows_ref, table_ref, image_ref, measured_ref, dual_ref, edge_ref, rim_ref,
    moved_ref, energy_ref, flat_ref, next_ref, plain_ref,
):
    slots = slot_of_lane(16)
    quarters = []
    for q in range(4):
        start = 16 * q * BACK_TILES
        tiles = [in_ref[pl.ds(start + t, 16, stride=BACK_TILES), :] for t in range(BACK_TILES)]
        near, far = [], []
        for g in range(2):
            near += transpose_pieces([tiles[2 * x + g] for x in range(4)], slots)
            pairs = trade(tiles[8 + g], tiles[10 + g], 1, slots)
            far += [*pairs, *(turn(value, -2 * PIECE) for value in pairs)]
        near += trade(*trade(tiles[12], tiles[13], 2, slots), 1, slots)
        far += trade(tiles[14], turn(tiles[14], -2 * PIECE), 1, slots)
        columns = [jnp.concatenate(near, axis=0), jnp.concatenate(far, axis=0)]
        quarters.append(jnp.concatenate(columns, axis=1))
    back = backward(table_ref, quarters)
    flat_ref[:, FULL:, :] = jnp.zeros((2, WIDE - FULL, LANES), jnp.float32)
    for r in range(4):
        for column in range(2):
            flat_ref[column, pl.ds(r, 80, stride=4), :] = back[r][
                :, column * LANES : (column + 1) * LANES
            ]
    back = jnp.concatenate([flat_ref[0].T, flat_ref[1].T], axis=0)[:, :FULL]

    def over_coils(value):
        half = value[:8] + value[8:]
        quarter = half[:4] + half[4:]
        return quarter[:2] + quarter[2:]

    for part in range(2):
        plain_ref[12 + part, :2, :FULL] = rim_ref[part, 0]
        for j in range(COILS):
            row = part * PIECE + 2 * j
            next_ref[row : row + 2, :] = edge_ref[10 + 2 * j + part, 0]
    for source, at, count in ((image_ref, 0, 2), (measured_ref, 2, 2), (dual_ref, 4, 6)):
        for channel in range(count):
            for x in range(ROWS):
                plain_ref[at + channel, 2 * x : 2 * x + 2, :FULL] = source[0, channel, x]
            plain_ref[at + channel, 2 * ROWS : 2 * ROWS + 2, :FULL] = edge_ref[at + channel, 0]
    for x in range(ROWS + 1):
        if x < ROWS:
            at = 2 * x * PIECE
            sr, si = rows_ref[at : at + PIECE, :], rows_ref[at + PIECE : at + 2 * PIECE, :]
        else:
            sr, si = next_ref[:PIECE, :], next_ref[PIECE:, :]
        at = x // 4 * LANES + x % 4 * PIECE
        br, bi = back[at : at + PIECE], back[at + 64 : at + 64 + PIECE]
        plain_ref[10, 2 * x : 2 * x + 2, :FULL] = over_coils(sr * br + si * bi)
        plain_ref[11, 2 * x : 2 * x + 2, :FULL] = over_coils(sr * bi - si * br)

    row = lax.broadcasted_iota(jnp.int32, (16, WIDE), 0)
    lane = lax.broadcasted_iota(jnp.int32, (16, WIDE), 1)
    known = (lane < FULL) & (row < 2 * ROWS + 2)
    inner_y = lane < FULL - 1
    inner_z = row % 2 == 0
    inner_x = row < jnp.where(last_ref[0] > 0, 2 * ROWS - 2, 16)

    def field(at):
        return jnp.where(known, plain_ref[at], 0.0)

    moved = [None] * 6
    for part in range(2):
        own, across, through = field(4 + part), field(6 + part), field(8 + part)
        masked_x = jnp.where(inner_x, own, 0.0)
        masked_y = jnp.where(inner_y, across, 0.0)
        masked_z = jnp.where(inner_z, through, 0.0)
        before = jnp.where(row < 2, field(12 + part), pltpu.roll(masked_x, 2, 0))
        adjoint = (before - masked_x) + (pltpu.roll(masked_y, 1, 1) - masked_y)
        adjoint = adjoint + (pltpu.roll(masked_z, 1, 0) - masked_z)
        now = field(part)
        new = now - 0.2 * (field(10 + part) - field(2 + part) + adjoint)
        extra = 2.0 * new - now
        grad_x = jnp.where(inner_x, pltpu.roll(extra, 14, 0) - extra, 0.0)
        grad_y = jnp.where(inner_y, pltpu.roll(extra, WIDE - 1, 1) - extra, 0.0)
        grad_z = jnp.where(inner_z, pltpu.roll(extra, 15, 0) - extra, 0.0)
        moved[part] = own + 0.5 * grad_x
        moved[2 + part] = across + 0.5 * grad_y
        moved[4 + part] = through + 0.5 * grad_z
        moved_ref[6 + part] = new
    energy = sum(value * value for value in moved)
    for channel in range(6):
        moved_ref[channel] = moved[channel]
    for copy in range(energy_ref.shape[0]):
        for t in range(3):
            energy_ref[copy, 10 * t : 10 * t + 10, :] = energy[:10, t * LANES : (t + 1) * LANES]


def last_kernel(limit, energy_ref, moved_ref, new_ref, out_ref):
    energy = energy_ref[0]
    for at in range(1, energy_ref.shape[0]):
        energy = energy + energy_ref[at]
    scale = 1.0 / jnp.maximum(1.0, jnp.sqrt(energy) / limit)
    scale = jnp.concatenate([scale[10 * t : 10 * t + 10] for t in range(3)], axis=1)
    for channel in range(6):
        value = moved_ref[channel][:10] * scale
        for x in range(ROWS):
            out_ref[0, channel, x] = value[2 * x : 2 * x + 2, :FULL]
    for part in range(2):
        for x in range(ROWS):
            new_ref[0, part, x] = moved_ref[6 + part, 2 * x : 2 * x + 2, :FULL]


PARAMS = pltpu.CompilerParams(vmem_limit_bytes=32 * 2**20)


def exchange(value):
    tiles = value.shape[0] // SLABS
    blocks = value.reshape(SLABS, 1, tiles * LANES)
    return lax.all_to_all(blocks, "slab", 0, 0, tiled=True).reshape(SLABS * tiles, LANES)


def shifted(value, axis, by):
    count = lax.axis_size(axis)
    pairs = [(i, i + by) for i in range(count) if 0 <= i + by < count]
    return lax.ppermute(value, axis, pairs)


def local(image, dual, adjoint_data, sens, kern):
    image, dual, adjoint_data, sens = (
        jnp.swapaxes(value, 2, 3) for value in (image, dual, adjoint_data, sens)
    )
    first, second, third, spread = tables()
    contrasts = lax.axis_size("con")
    weight = pl.pallas_call(
        weight_kernel,
        out_shape=jax.ShapeDtypeStruct((PADDED, WIDE), jnp.float32),
        compiler_params=PARAMS,
        name="weights",
    )(kern, spread)
    whole = pl.BlockSpec(memory_space=pltpu.HBM)
    bands = pl.pallas_call(
        first_kernel,
        in_specs=[whole] * 3,
        out_shape=jax.ShapeDtypeStruct((SLABS * TILES, LANES), jnp.float32),
        scratch_shapes=[
            pltpu.VMEM(image.shape, jnp.float32),
            pltpu.VMEM(sens.shape, jnp.float32),
            pltpu.VMEM(first.shape, jnp.bfloat16),
            pltpu.VMEM((2, WIDE, LANES), jnp.float32),
            pltpu.VMEM((2 * ROWS * PIECE, FULL), jnp.float32),
            pltpu.SemaphoreType.DMA((6,)),
        ],
        compiler_params=PARAMS,
        name="first",
    )(*(pltpu.with_memory_space_constraint(v, pltpu.HBM) for v in (image, sens, first)))
    edge, rim, sens_rows = pl.pallas_call(
        edge_kernel,
        out_shape=(
            jax.ShapeDtypeStruct((10 + 2 * COILS, 1, PLANES, FULL), jnp.float32),
            jax.ShapeDtypeStruct((2, 1, PLANES, FULL), jnp.float32),
            jax.ShapeDtypeStruct((2 * ROWS * PIECE, FULL), jnp.float32),
        ),
        compiler_params=PARAMS,
        name="edge",
    )(image, adjoint_data, dual, sens)
    edge = shifted(edge, "slab", -1)
    rim = shifted(rim, "slab", 1)
    is_last = (lax.axis_index("slab") == SLABS - 1).astype(jnp.int32).reshape(1)
    bands, edge, rim, is_last, sens_rows = lax.optimization_barrier(
        (exchange(bands), edge, rim, is_last, sens_rows)
    )
    returned = pl.pallas_call(
        second_kernel,
        out_shape=jax.ShapeDtypeStruct((SLABS * BACK_TILES, LANES), jnp.float32),
        compiler_params=PARAMS,
        name="second",
    )(bands, weight, second)
    moved, energy = pl.pallas_call(
        third_kernel,
        in_specs=[pl.BlockSpec(memory_space=pltpu.SMEM)]
        + [pl.BlockSpec(memory_space=pltpu.VMEM)] * 8,
        out_shape=(
            jax.ShapeDtypeStruct((8, 16, WIDE), jnp.float32),
            jax.ShapeDtypeStruct((contrasts, 30, LANES), jnp.float32),
        ),
        scratch_shapes=[
            pltpu.VMEM((2, WIDE, LANES), jnp.float32),
            pltpu.VMEM((2 * PIECE, FULL), jnp.float32),
            pltpu.VMEM((14, 16, WIDE), jnp.float32),
        ],
        compiler_params=PARAMS,
        name="third",
    )(is_last, exchange(returned), sens_rows, third, image, adjoint_data, dual, edge, rim)
    new_image, new_dual = pl.pallas_call(
        functools.partial(last_kernel, 0.9 * math.sqrt(6.0 * contrasts)),
        out_shape=(
            jax.ShapeDtypeStruct(image.shape, jnp.float32),
            jax.ShapeDtypeStruct(dual.shape, jnp.float32),
        ),
        compiler_params=PARAMS,
        name="last",
    )(lax.all_to_all(energy, "con", 0, 0, tiled=True), moved)
    return jnp.swapaxes(new_image, 2, 3), jnp.swapaxes(new_dual, 2, 3)


def solution(mesh):
    return jax.shard_map(
        local,
        mesh=mesh,
        in_specs=(
            P("con", None, None, "slab", None),
            P("con", None, None, "slab", None),
            P("con", None, None, "slab", None),
            P(None, None, None, "slab", None),
            P("con", "slab", None),
        ),
        out_specs=(P("con", None, None, "slab", None), P("con", None, None, "slab", None)),
        check_vma=False,
    )
```

```python
import functools
import math

import jax
import jax.numpy as jnp
import ml_dtypes
import numpy as np
from jax import lax
from jax.experimental import pallas as pl
from jax.experimental.pallas import tpu as pltpu
from jax.sharding import PartitionSpec as P

FULL = 320
PADDED = 640
QUARTER = 160
SLABS = 64
ROWS = 5
BAND = 10
COILS = 8
PLANES = 2
PIECE = PLANES * COILS
TILES = 13
BACK_TILES = 15
LANES = 128
WIDE = 384
PACKED = 25


def tile_of(x, b, rows):
    if b < 8:
        return 2 * x + b // 4, b % 4
    return 2 * rows + x // 2, (x % 2) * 2 + b - 8


def split(value):
    high = value.astype(jnp.bfloat16)
    return high, (value - high.astype(jnp.float32)).astype(jnp.bfloat16)


def np_split(value):
    high = value.astype(np.float32).astype(ml_dtypes.bfloat16)
    low = (value - high.astype(np.float64)).astype(np.float32).astype(ml_dtypes.bfloat16)
    return high, low


def stack_depth(value):
    high, low = np_split(value)
    return np.concatenate([high, high, low], axis=-1)


@functools.cache
def tables():
    low = np.arange(QUARTER)
    by_band = (np.arange(BAND)[:, None] + BAND * np.arange(16)[None, :]).reshape(-1)
    points_y = [4 * np.arange(80) + r for r in range(4)]
    points_x = []
    for r in range(4):
        order = [5 * (4 * u + (r - x) % 4) + x for x in range(ROWS) for u in range(16)]
        points_x.append(np.array(order))

    def stack(points, k):
        result = []
        for point in points:
            angle = 2 * np.pi * (k[:, None] * point[None, :] % PADDED) / PADDED
            result.append(np.concatenate([np.cos(angle), np.sin(angle)], axis=1))
        return np.stack(result)

    along_y = stack(points_y, by_band)
    along_x = stack(points_x, low)
    back_x = along_x.transpose(0, 2, 1)
    back_y = along_y.transpose(0, 2, 1) / PADDED**2
    spread = np.zeros((BAND, WIDE), np.float32)
    for b in range(BAND):
        for part in range(2):
            at = b // 4 * LANES + part * 64 + b % 4 * PIECE
            spread[b, at : at + PIECE] = 1.0
    first, back_y = stack_depth(along_y), stack_depth(back_y)
    second = np.stack([stack_depth(along_x), stack_depth(back_x)])
    return first, second, back_y, spread.astype(ml_dtypes.bfloat16)


def dot(left, right):
    return jnp.dot(left, right, preferred_element_type=jnp.float32)


def dot3(left, right):
    high, low = split(right)
    return dot(left, jnp.concatenate([high, low, high], axis=0))


def turn(value, shift):
    shift %= LANES
    return value if shift == 0 else pltpu.roll(value, shift, 1)


def slot_of_lane(rows):
    return lax.broadcasted_iota(jnp.int32, (rows, LANES), 1) % 64 // PIECE


def gather_pieces(sources, slots):
    result = None
    for at, source in enumerate(sources):
        if source is None:
            continue
        moved = turn(source[0], PIECE * (at - source[1]))
        result = moved if result is None else jnp.where(slots == at, moved, result)
    return result


def trade(left, right, step, slots):
    low = slots // step % 2 == 0
    shift = PIECE * step
    return jnp.where(low, left, turn(right, shift)), jnp.where(low, turn(left, -shift), right)


def transpose_pieces(tiles, slots):
    a0, a1 = trade(tiles[0], tiles[1], 1, slots)
    a2, a3 = trade(tiles[2], tiles[3], 1, slots)
    b0, b2 = trade(a0, a2, 2, slots)
    b1, b3 = trade(a1, a3, 2, slots)
    return b0, b1, b2, b3


def times_minus_i(value):
    rows = value.shape[0]
    is_real = lax.broadcasted_iota(jnp.int32, (rows, LANES), 1) < 64
    parts = []
    for at in range(0, value.shape[1], LANES):
        turned = turn(value[:, at : at + LANES], 64)
        parts.append(jnp.where(is_real, turned, -turned))
    return jnp.concatenate(parts, axis=1)


def butterfly(a0, a1, a2, a3):
    even, odd = a0 + a2, a1 + a3
    apart, turned = a0 - a2, times_minus_i(a1 - a3)
    return even + odd, apart + turned, even - odd, apart - turned


def forward(table, residues):
    parts = []
    for r in range(4):
        data = jnp.concatenate([residues[r], times_minus_i(residues[r])], axis=0)
        parts.append(dot3(table[r], data))
    return butterfly(*parts)


def backward(table, quarters):
    sums = butterfly(*quarters)
    result = []
    for r, at in enumerate((0, 3, 2, 1)):
        both = dot3(table[r], sums[at])
        result.append(both[:80] - times_minus_i(both[80:]))
    return result


def gather_rows(sens_ref, rows_ref):
    for x in range(ROWS):
        for part in range(2):
            for j in range(COILS):
                row = (2 * x + part) * PIECE + 2 * j
                rows_ref[row : row + 2, :] = sens_ref[j, part, x]


def first_kernel(
    image_hbm, sens_hbm, table_hbm, out_ref,
    image_ref, sens_ref, table_ref, flat_ref, rows_ref, sems,
):
    copies = [
        pltpu.make_async_copy(sens_hbm, sens_ref, sems.at[0]),
        pltpu.make_async_copy(image_hbm, image_ref, sems.at[1]),
    ]
    for r in range(4):
        copies.append(pltpu.make_async_copy(table_hbm.at[r], table_ref.at[r], sems.at[2 + r]))
    for copy in copies:
        copy.start()
    copies[0].wait()
    gather_rows(sens_ref, rows_ref)
    copies[1].wait()
    real, imag = [], []
    for x in range(ROWS):
        sr = rows_ref[2 * x * PIECE : (2 * x + 1) * PIECE, :]
        si = rows_ref[(2 * x + 1) * PIECE : (2 * x + 2) * PIECE, :]
        ur = jnp.concatenate([image_ref[0, 0, x]] * COILS, axis=0)
        ui = jnp.concatenate([image_ref[0, 1, x]] * COILS, axis=0)
        real.append(sr * ur - si * ui)
        imag.append(sr * ui + si * ur)
    rest = [jnp.zeros((3 * PIECE, FULL), jnp.float32)]
    coil = jnp.concatenate(real[:4] + imag[:4] + real[4:] + rest + imag[4:] + rest, axis=0)
    coil = jnp.concatenate([coil, jnp.zeros((256, WIDE - FULL), jnp.float32)], axis=1).T
    flat_ref[0] = coil[:, :LANES]
    flat_ref[1] = coil[:, LANES:]
    residues = []
    for r in range(4):
        columns = [flat_ref[column, pl.ds(r, 80, stride=4), :] for column in range(2)]
        residues.append(jnp.concatenate(columns, axis=1))

    for r in range(4):
        copies[2 + r].wait()
    bands = forward(table_ref, residues)
    slots = slot_of_lane(16)
    for q in range(4):
        start = 16 * q * TILES

        def put(t, value):
            out_ref[pl.ds(start + t, 16, stride=TILES), :] = value

        near = [bands[q][b * 16 : (b + 1) * 16, :LANES] for b in range(BAND)]
        far = [bands[q][b * 16 : (b + 1) * 16, LANES:] for b in range(BAND)]
        for g in range(2):
            for x, value in enumerate(transpose_pieces(near[4 * g : 4 * g + 4], slots)):
                put(2 * x + g, value)
            put(8 + g, gather_pieces([(far[4 * g + i], 0) for i in range(4)], slots))
        for pair, value in enumerate(trade(*trade(near[8], near[9], 1, slots), 2, slots)):
            put(10 + pair, value)
        put(12, gather_pieces([(far[8], 0), (far[9], 0)], slots))


def weight_kernel(kern_ref, spread_ref, out_ref):
    form = (((0,), (0,)), ((), ()))
    high, low = split(kern_ref[0])
    out_ref[...] = lax.dot_general(
        high, spread_ref[...], form, preferred_element_type=jnp.float32
    ) + lax.dot_general(low, spread_ref[...], form, preferred_element_type=jnp.float32)


def edge_kernel(image_ref, measured_ref, dual_ref, sens_ref, edge_ref, rim_ref, rows_ref):
    gather_rows(sens_ref, rows_ref)
    for at, count, source in ((0, 2, image_ref), (2, 2, measured_ref), (4, 6, dual_ref)):
        for channel in range(count):
            edge_ref[at + channel, 0] = source[0, channel, 0]
    for j in range(COILS):
        for part in range(2):
            edge_ref[10 + 2 * j + part, 0] = sens_ref[j, part, 0]
    for part in range(2):
        rim_ref[part, 0] = dual_ref[0, part, ROWS - 1]


def second_kernel(in_ref, weight_ref, table_ref, out_ref):
    def place(x, r, t):
        return pl.ds((r - x) % 4 * TILES + t, 16, stride=4 * TILES)

    residues = []
    for r in range(4):
        rows = []
        for x in range(ROWS):
            rest = turn(in_ref[place(x, r, 10 + x // 2), :], -2 * PIECE * (x % 2))
            whole = [in_ref[place(x, r, 2 * x), :], in_ref[place(x, r, 2 * x + 1), :]]
            rows.append(jnp.concatenate(whole + [rest], axis=1))
        residues.append(jnp.concatenate(rows, axis=0))
    spectrum = forward(table_ref.at[0], residues)
    weighted = [
        part * weight_ref[q * QUARTER : (q + 1) * QUARTER, :] for q, part in enumerate(spectrum)
    ]
    result = backward(table_ref.at[1], weighted)
    lower = slot_of_lane(16) < 2
    for s in range(4):

        def put(t, value):
            out_ref[pl.ds(s * BACK_TILES + t, 16, stride=4 * BACK_TILES), :] = value

        rows = [result[(s + x) % 4][x * 16 : (x + 1) * 16] for x in range(ROWS)]
        following = result[(s + 1) % 4][:16]
        rows.append(pltpu.roll(following, 15, 0) if s == 3 else following)
        for x in range(ROWS + 1):
            for g in range(2):
                put(2 * x + g, rows[x][:, g * LANES : (g + 1) * LANES])
        for pair in range(3):
            left, right = rows[2 * pair][:, 2 * LANES :], rows[2 * pair + 1][:, 2 * LANES :]
            put(12 + pair, jnp.where(lower, left, turn(right, 2 * PIECE)))


def third_kernel(
    last_ref, in_ref, rows_ref, table_ref, image_ref, measured_ref, dual_ref, edge_ref, rim_ref,
    moved_ref, energy_ref, flat_ref, next_ref, plain_ref,
):
    slots = slot_of_lane(16)
    quarters = []
    for q in range(4):
        start = 16 * q * BACK_TILES
        tiles = [in_ref[pl.ds(start + t, 16, stride=BACK_TILES), :] for t in range(BACK_TILES)]
        near, far = [], []
        for g in range(2):
            near += transpose_pieces([tiles[2 * x + g] for x in range(4)], slots)
            pairs = trade(tiles[8 + g], tiles[10 + g], 1, slots)
            far += [*pairs, *(turn(value, -2 * PIECE) for value in pairs)]
        near += trade(*trade(tiles[12], tiles[13], 2, slots), 1, slots)
        far += trade(tiles[14], turn(tiles[14], -2 * PIECE), 1, slots)
        columns = [jnp.concatenate(near, axis=0), jnp.concatenate(far, axis=0)]
        quarters.append(jnp.concatenate(columns, axis=1))
    back = backward(table_ref, quarters)
    flat_ref[:, FULL:, :] = jnp.zeros((2, WIDE - FULL, LANES), jnp.float32)
    for r in range(4):
        for column in range(2):
            flat_ref[column, pl.ds(r, 80, stride=4), :] = back[r][
                :, column * LANES : (column + 1) * LANES
            ]
    back = jnp.concatenate([flat_ref[0].T, flat_ref[1].T], axis=0)[:, :FULL]

    def over_coils(value):
        half = value[:8] + value[8:]
        quarter = half[:4] + half[4:]
        return quarter[:2] + quarter[2:]

    for part in range(2):
        plain_ref[12 + part, :2, :FULL] = rim_ref[part, 0]
        for j in range(COILS):
            row = part * PIECE + 2 * j
            next_ref[row : row + 2, :] = edge_ref[10 + 2 * j + part, 0]
    for source, at, count in ((image_ref, 0, 2), (measured_ref, 2, 2), (dual_ref, 4, 6)):
        for channel in range(count):
            for x in range(ROWS):
                plain_ref[at + channel, 2 * x : 2 * x + 2, :FULL] = source[0, channel, x]
            plain_ref[at + channel, 2 * ROWS : 2 * ROWS + 2, :FULL] = edge_ref[at + channel, 0]
    for x in range(ROWS + 1):
        if x < ROWS:
            at = 2 * x * PIECE
            sr, si = rows_ref[at : at + PIECE, :], rows_ref[at + PIECE : at + 2 * PIECE, :]
        else:
            sr, si = next_ref[:PIECE, :], next_ref[PIECE:, :]
        at = x // 4 * LANES + x % 4 * PIECE
        br, bi = back[at : at + PIECE], back[at + 64 : at + 64 + PIECE]
        plain_ref[10, 2 * x : 2 * x + 2, :FULL] = over_coils(sr * br + si * bi)
        plain_ref[11, 2 * x : 2 * x + 2, :FULL] = over_coils(sr * bi - si * br)

    row = lax.broadcasted_iota(jnp.int32, (16, WIDE), 0)
    lane = lax.broadcasted_iota(jnp.int32, (16, WIDE), 1)
    known = (lane < FULL) & (row < 2 * ROWS + 2)
    inner_y = lane < FULL - 1
    inner_z = row % 2 == 0
    inner_x = row < jnp.where(last_ref[0] > 0, 2 * ROWS - 2, 16)

    def field(at):
        return jnp.where(known, plain_ref[at], 0.0)

    moved = [None] * 6
    for part in range(2):
        own, across, through = field(4 + part), field(6 + part), field(8 + part)
        masked_x = jnp.where(inner_x, own, 0.0)
        masked_y = jnp.where(inner_y, across, 0.0)
        masked_z = jnp.where(inner_z, through, 0.0)
        before = jnp.where(row < 2, field(12 + part), pltpu.roll(masked_x, 2, 0))
        adjoint = (before - masked_x) + (pltpu.roll(masked_y, 1, 1) - masked_y)
        adjoint = adjoint + (pltpu.roll(masked_z, 1, 0) - masked_z)
        now = field(part)
        new = now - 0.2 * (field(10 + part) - field(2 + part) + adjoint)
        extra = 2.0 * new - now
        grad_x = jnp.where(inner_x, pltpu.roll(extra, 14, 0) - extra, 0.0)
        grad_y = jnp.where(inner_y, pltpu.roll(extra, WIDE - 1, 1) - extra, 0.0)
        grad_z = jnp.where(inner_z, pltpu.roll(extra, 15, 0) - extra, 0.0)
        moved[part] = own + 0.5 * grad_x
        moved[2 + part] = across + 0.5 * grad_y
        moved[4 + part] = through + 0.5 * grad_z
        moved_ref[6 + part] = new
    energy = sum(value * value for value in moved)
    for channel in range(6):
        moved_ref[channel] = moved[channel]
    rest = energy[:, 2 * LANES :]
    rest = jnp.where(lane[:5, :LANES] < 64, rest[:5], turn(rest, 64)[5:10])
    packed = jnp.concatenate([energy[:10, :LANES], energy[:10, LANES : 2 * LANES], rest], axis=0)
    for at in range(0, energy_ref.shape[0], PACKED):
        energy_ref[at : at + PACKED, :] = packed


def last_kernel(limit, energy_ref, moved_ref, new_ref, out_ref):
    energy = energy_ref[:PACKED, :]
    for at in range(PACKED, energy_ref.shape[0], PACKED):
        energy = energy + energy_ref[at : at + PACKED, :]
    scale = 1.0 / jnp.maximum(1.0, jnp.sqrt(energy) / limit)
    rest = jnp.concatenate([scale[20:], turn(scale[20:], 64)], axis=0)
    scale = jnp.concatenate([scale[:10], scale[10:20], rest], axis=1)
    for channel in range(6):
        value = moved_ref[channel][:10] * scale
        for x in range(ROWS):
            out_ref[0, channel, x] = value[2 * x : 2 * x + 2, :FULL]
    for part in range(2):
        for x in range(ROWS):
            new_ref[0, part, x] = moved_ref[6 + part, 2 * x : 2 * x + 2, :FULL]


PARAMS = pltpu.CompilerParams(vmem_limit_bytes=32 * 2**20)


def exchange(value, axis, count):
    blocks = value.reshape(count, 1, -1)
    return lax.all_to_all(blocks, axis, 0, 0, tiled=True).reshape(value.shape)


def shifted(value, axis, by):
    count = lax.axis_size(axis)
    pairs = [(i, i + by) for i in range(count) if 0 <= i + by < count]
    return lax.ppermute(value, axis, pairs)


def local(image, dual, adjoint_data, sens, kern):
    image, dual, adjoint_data, sens = (
        jnp.swapaxes(value, 2, 3) for value in (image, dual, adjoint_data, sens)
    )
    first, second, third, spread = tables()
    contrasts = lax.axis_size("con")
    weight = pl.pallas_call(
        weight_kernel,
        out_shape=jax.ShapeDtypeStruct((PADDED, WIDE), jnp.float32),
        compiler_params=PARAMS,
        name="weights",
    )(kern, spread)
    whole = pl.BlockSpec(memory_space=pltpu.HBM)
    bands = pl.pallas_call(
        first_kernel,
        in_specs=[whole] * 3,
        out_shape=jax.ShapeDtypeStruct((SLABS * TILES, LANES), jnp.float32),
        scratch_shapes=[
            pltpu.VMEM(image.shape, jnp.float32),
            pltpu.VMEM(sens.shape, jnp.float32),
            pltpu.VMEM(first.shape, jnp.bfloat16),
            pltpu.VMEM((2, WIDE, LANES), jnp.float32),
            pltpu.VMEM((2 * ROWS * PIECE, FULL), jnp.float32),
            pltpu.SemaphoreType.DMA((6,)),
        ],
        compiler_params=PARAMS,
        name="first",
    )(*(pltpu.with_memory_space_constraint(v, pltpu.HBM) for v in (image, sens, first)))
    edge, rim, sens_rows = pl.pallas_call(
        edge_kernel,
        out_shape=(
            jax.ShapeDtypeStruct((10 + 2 * COILS, 1, PLANES, FULL), jnp.float32),
            jax.ShapeDtypeStruct((2, 1, PLANES, FULL), jnp.float32),
            jax.ShapeDtypeStruct((2 * ROWS * PIECE, FULL), jnp.float32),
        ),
        compiler_params=PARAMS,
        name="edge",
    )(image, adjoint_data, dual, sens)
    edge = shifted(edge, "slab", -1)
    rim = shifted(rim, "slab", 1)
    is_last = (lax.axis_index("slab") == SLABS - 1).astype(jnp.int32).reshape(1)
    bands, edge, rim, is_last, sens_rows = lax.optimization_barrier(
        (exchange(bands, "slab", SLABS), edge, rim, is_last, sens_rows)
    )
    returned = pl.pallas_call(
        second_kernel,
        out_shape=jax.ShapeDtypeStruct((SLABS * BACK_TILES, LANES), jnp.float32),
        compiler_params=PARAMS,
        name="second",
    )(bands, weight, second)
    moved, energy = pl.pallas_call(
        third_kernel,
        in_specs=[pl.BlockSpec(memory_space=pltpu.SMEM)]
        + [pl.BlockSpec(memory_space=pltpu.VMEM)] * 8,
        out_shape=(
            jax.ShapeDtypeStruct((8, 16, WIDE), jnp.float32),
            jax.ShapeDtypeStruct((contrasts * PACKED, LANES), jnp.float32),
        ),
        scratch_shapes=[
            pltpu.VMEM((2, WIDE, LANES), jnp.float32),
            pltpu.VMEM((2 * PIECE, FULL), jnp.float32),
            pltpu.VMEM((14, 16, WIDE), jnp.float32),
        ],
        compiler_params=PARAMS,
        name="third",
    )(is_last, exchange(returned, "slab", SLABS), sens_rows, third, image, adjoint_data, dual, edge, rim)
    new_image, new_dual = pl.pallas_call(
        functools.partial(last_kernel, 0.9 * math.sqrt(6.0 * contrasts)),
        out_shape=(
            jax.ShapeDtypeStruct(image.shape, jnp.float32),
            jax.ShapeDtypeStruct(dual.shape, jnp.float32),
        ),
        compiler_params=PARAMS,
        name="last",
    )(exchange(energy, "con", contrasts), moved)
    return jnp.swapaxes(new_image, 2, 3), jnp.swapaxes(new_dual, 2, 3)


def solution(mesh):
    return jax.shard_map(
        local,
        mesh=mesh,
        in_specs=(
            P("con", None, None, "slab", None),
            P("con", None, None, "slab", None),
            P("con", None, None, "slab", None),
            P(None, None, None, "slab", None),
            P("con", "slab", None),
        ),
        out_specs=(P("con", None, None, "slab", None), P("con", None, None, "slab", None)),
        check_vma=False,
    )
```

```python
import functools
import math

import jax
import jax.numpy as jnp
import ml_dtypes
import numpy as np
from jax import lax
from jax.experimental import pallas as pl
from jax.experimental.pallas import tpu as pltpu
from jax.sharding import PartitionSpec as P

FULL = 320
PADDED = 640
QUARTER = 160
SLABS = 64
ROWS = 5
BAND = 10
COILS = 8
PLANES = 2
PIECE = PLANES * COILS
TILES = 13
BACK_TILES = 15
LANES = 128
WIDE = 384


def tile_of(x, b, rows):
    if b < 8:
        return 2 * x + b // 4, b % 4
    return 2 * rows + x // 2, (x % 2) * 2 + b - 8


def split(value):
    high = value.astype(jnp.bfloat16)
    return high, (value - high.astype(jnp.float32)).astype(jnp.bfloat16)


def np_split(value):
    high = value.astype(np.float32).astype(ml_dtypes.bfloat16)
    low = (value - high.astype(np.float64)).astype(np.float32).astype(ml_dtypes.bfloat16)
    return high, low


def stack_depth(value):
    high, low = np_split(value)
    return np.concatenate([high, high, low], axis=-1)


@functools.cache
def tables():
    low = np.arange(QUARTER)
    by_band = (np.arange(BAND)[:, None] + BAND * np.arange(16)[None, :]).reshape(-1)
    points_y = [4 * np.arange(80) + r for r in range(4)]
    points_x = []
    for r in range(4):
        order = [5 * (4 * u + (r - x) % 4) + x for x in range(ROWS) for u in range(16)]
        points_x.append(np.array(order))

    def stack(points, k):
        result = []
        for point in points:
            angle = 2 * np.pi * (k[:, None] * point[None, :] % PADDED) / PADDED
            result.append(np.concatenate([np.cos(angle), np.sin(angle)], axis=1))
        return np.stack(result)

    along_y = stack(points_y, by_band)
    along_x = stack(points_x, low)
    back_x = along_x.transpose(0, 2, 1)
    back_y = along_y.transpose(0, 2, 1) / PADDED**2
    spread = np.zeros((BAND, WIDE), np.float32)
    for b in range(BAND):
        for part in range(2):
            at = b // 4 * LANES + part * 64 + b % 4 * PIECE
            spread[b, at : at + PIECE] = 1.0
    first, back_y = stack_depth(along_y), stack_depth(back_y)
    second = np.stack([stack_depth(along_x), stack_depth(back_x)])
    return first, second, back_y, spread.astype(ml_dtypes.bfloat16)


def dot(left, right):
    return jnp.dot(left, right, preferred_element_type=jnp.float32)


def dot3(left, right):
    high, low = split(right)
    return dot(left, jnp.concatenate([high, low, high], axis=0))


def turn(value, shift):
    shift %= LANES
    return value if shift == 0 else pltpu.roll(value, shift, 1)


def slot_of_lane(rows):
    return lax.broadcasted_iota(jnp.int32, (rows, LANES), 1) % 64 // PIECE


def gather_pieces(sources, slots):
    result = None
    for at, source in enumerate(sources):
        if source is None:
            continue
        moved = turn(source[0], PIECE * (at - source[1]))
        result = moved if result is None else jnp.where(slots == at, moved, result)
    return result


def trade(left, right, step, slots):
    low = slots // step % 2 == 0
    shift = PIECE * step
    return jnp.where(low, left, turn(right, shift)), jnp.where(low, turn(left, -shift), right)


def transpose_pieces(tiles, slots):
    a0, a1 = trade(tiles[0], tiles[1], 1, slots)
    a2, a3 = trade(tiles[2], tiles[3], 1, slots)
    b0, b2 = trade(a0, a2, 2, slots)
    b1, b3 = trade(a1, a3, 2, slots)
    return b0, b1, b2, b3


def times_minus_i(value):
    rows = value.shape[0]
    is_real = lax.broadcasted_iota(jnp.int32, (rows, LANES), 1) < 64
    parts = []
    for at in range(0, value.shape[1], LANES):
        turned = turn(value[:, at : at + LANES], 64)
        parts.append(jnp.where(is_real, turned, -turned))
    return jnp.concatenate(parts, axis=1)


def butterfly(a0, a1, a2, a3):
    even, odd = a0 + a2, a1 + a3
    apart, turned = a0 - a2, times_minus_i(a1 - a3)
    return even + odd, apart + turned, even - odd, apart - turned


def forward(table, residues):
    parts = []
    for r in range(4):
        data = jnp.concatenate([residues[r], times_minus_i(residues[r])], axis=0)
        parts.append(dot3(table[r], data))
    return butterfly(*parts)


def backward(table, quarters):
    sums = butterfly(*quarters)
    result = []
    for r, at in enumerate((0, 3, 2, 1)):
        both = dot3(table[r], sums[at])
        result.append(both[:80] - times_minus_i(both[80:]))
    return result


def gather_rows(sens_ref, rows_ref):
    for x in range(ROWS):
        for part in range(2):
            for j in range(COILS):
                row = (2 * x + part) * PIECE + 2 * j
                rows_ref[row : row + 2, :] = sens_ref[j, part, x]


def first_kernel(
    image_hbm, sens_hbm, table_hbm, out_ref,
    image_ref, sens_ref, table_ref, flat_ref, rows_ref, sems,
):
    copies = [
        pltpu.make_async_copy(sens_hbm, sens_ref, sems.at[0]),
        pltpu.make_async_copy(image_hbm, image_ref, sems.at[1]),
    ]
    for r in range(4):
        copies.append(pltpu.make_async_copy(table_hbm.at[r], table_ref.at[r], sems.at[2 + r]))
    for copy in copies:
        copy.start()
    copies[0].wait()
    gather_rows(sens_ref, rows_ref)
    copies[1].wait()
    real, imag = [], []
    for x in range(ROWS):
        sr = rows_ref[2 * x * PIECE : (2 * x + 1) * PIECE, :]
        si = rows_ref[(2 * x + 1) * PIECE : (2 * x + 2) * PIECE, :]
        ur = jnp.concatenate([image_ref[0, 0, x]] * COILS, axis=0)
        ui = jnp.concatenate([image_ref[0, 1, x]] * COILS, axis=0)
        real.append(sr * ur - si * ui)
        imag.append(sr * ui + si * ur)
    rest = [jnp.zeros((3 * PIECE, FULL), jnp.float32)]
    coil = jnp.concatenate(real[:4] + imag[:4] + real[4:] + rest + imag[4:] + rest, axis=0)
    coil = jnp.concatenate([coil, jnp.zeros((256, WIDE - FULL), jnp.float32)], axis=1).T
    flat_ref[0] = coil[:, :LANES]
    flat_ref[1] = coil[:, LANES:]
    residues = []
    for r in range(4):
        columns = [flat_ref[column, pl.ds(r, 80, stride=4), :] for column in range(2)]
        residues.append(jnp.concatenate(columns, axis=1))

    for r in range(4):
        copies[2 + r].wait()
    bands = forward(table_ref, residues)
    slots = slot_of_lane(16)
    for q in range(4):
        start = 16 * q * TILES

        def put(t, value):
            out_ref[pl.ds(start + t, 16, stride=TILES), :] = value

        near = [bands[q][b * 16 : (b + 1) * 16, :LANES] for b in range(BAND)]
        far = [bands[q][b * 16 : (b + 1) * 16, LANES:] for b in range(BAND)]
        for g in range(2):
            for x, value in enumerate(transpose_pieces(near[4 * g : 4 * g + 4], slots)):
                put(2 * x + g, value)
            put(8 + g, gather_pieces([(far[4 * g + i], 0) for i in range(4)], slots))
        for pair, value in enumerate(trade(*trade(near[8], near[9], 1, slots), 2, slots)):
            put(10 + pair, value)
        put(12, gather_pieces([(far[8], 0), (far[9], 0)], slots))


def weight_kernel(kern_ref, spread_ref, out_ref):
    form = (((0,), (0,)), ((), ()))
    high, low = split(kern_ref[0])
    out_ref[...] = lax.dot_general(
        high, spread_ref[...], form, preferred_element_type=jnp.float32
    ) + lax.dot_general(low, spread_ref[...], form, preferred_element_type=jnp.float32)


def edge_kernel(image_ref, measured_ref, dual_ref, sens_ref, edge_ref, rim_ref, rows_ref):
    gather_rows(sens_ref, rows_ref)
    for at, count, source in ((0, 2, image_ref), (2, 2, measured_ref), (4, 6, dual_ref)):
        for channel in range(count):
            edge_ref[at + channel, 0] = source[0, channel, 0]
    for j in range(COILS):
        for part in range(2):
            edge_ref[10 + 2 * j + part, 0] = sens_ref[j, part, 0]
    for part in range(2):
        rim_ref[part, 0] = dual_ref[0, part, ROWS - 1]


def second_kernel(in_ref, weight_ref, table_ref, out_ref):
    def place(x, r, t):
        return pl.ds((r - x) % 4 * TILES + t, 16, stride=4 * TILES)

    residues = []
    for r in range(4):
        rows = []
        for x in range(ROWS):
            rest = turn(in_ref[place(x, r, 10 + x // 2), :], -2 * PIECE * (x % 2))
            whole = [in_ref[place(x, r, 2 * x), :], in_ref[place(x, r, 2 * x + 1), :]]
            rows.append(jnp.concatenate(whole + [rest], axis=1))
        residues.append(jnp.concatenate(rows, axis=0))
    spectrum = forward(table_ref.at[0], residues)
    weighted = [
        part * weight_ref[q * QUARTER : (q + 1) * QUARTER, :] for q, part in enumerate(spectrum)
    ]
    result = backward(table_ref.at[1], weighted)
    lower = slot_of_lane(16) < 2
    for s in range(4):

        def put(t, value):
            out_ref[pl.ds(s * BACK_TILES + t, 16, stride=4 * BACK_TILES), :] = value

        rows = [result[(s + x) % 4][x * 16 : (x + 1) * 16] for x in range(ROWS)]
        following = result[(s + 1) % 4][:16]
        rows.append(pltpu.roll(following, 15, 0) if s == 3 else following)
        for x in range(ROWS + 1):
            for g in range(2):
                put(2 * x + g, rows[x][:, g * LANES : (g + 1) * LANES])
        for pair in range(3):
            left, right = rows[2 * pair][:, 2 * LANES :], rows[2 * pair + 1][:, 2 * LANES :]
            put(12 + pair, jnp.where(lower, left, turn(right, 2 * PIECE)))


def third_kernel(
    last_ref, in_ref, rows_ref, table_ref, image_ref, measured_ref, dual_ref, edge_ref, rim_ref,
    moved_ref, energy_ref, flat_ref, next_ref, plain_ref,
):
    slots = slot_of_lane(16)
    quarters = []
    for q in range(4):
        start = 16 * q * BACK_TILES
        tiles = [in_ref[pl.ds(start + t, 16, stride=BACK_TILES), :] for t in range(BACK_TILES)]
        near, far = [], []
        for g in range(2):
            near += transpose_pieces([tiles[2 * x + g] for x in range(4)], slots)
            pairs = trade(tiles[8 + g], tiles[10 + g], 1, slots)
            far += [*pairs, *(turn(value, -2 * PIECE) for value in pairs)]
        near += trade(*trade(tiles[12], tiles[13], 2, slots), 1, slots)
        far += trade(tiles[14], turn(tiles[14], -2 * PIECE), 1, slots)
        columns = [jnp.concatenate(near, axis=0), jnp.concatenate(far, axis=0)]
        quarters.append(jnp.concatenate(columns, axis=1))
    back = backward(table_ref, quarters)
    flat_ref[:, FULL:, :] = jnp.zeros((2, WIDE - FULL, LANES), jnp.float32)
    for r in range(4):
        for column in range(2):
            flat_ref[column, pl.ds(r, 80, stride=4), :] = back[r][
                :, column * LANES : (column + 1) * LANES
            ]
    back = jnp.concatenate([flat_ref[0].T, flat_ref[1].T], axis=0)[:, :FULL]

    def over_coils(value):
        half = value[:8] + value[8:]
        quarter = half[:4] + half[4:]
        return quarter[:2] + quarter[2:]

    for part in range(2):
        plain_ref[12 + part, :2, :FULL] = rim_ref[part, 0]
        for j in range(COILS):
            row = part * PIECE + 2 * j
            next_ref[row : row + 2, :] = edge_ref[10 + 2 * j + part, 0]
    for source, at, count in ((image_ref, 0, 2), (measured_ref, 2, 2), (dual_ref, 4, 6)):
        for channel in range(count):
            for x in range(ROWS):
                plain_ref[at + channel, 2 * x : 2 * x + 2, :FULL] = source[0, channel, x]
            plain_ref[at + channel, 2 * ROWS : 2 * ROWS + 2, :FULL] = edge_ref[at + channel, 0]
    for x in range(ROWS + 1):
        if x < ROWS:
            at = 2 * x * PIECE
            sr, si = rows_ref[at : at + PIECE, :], rows_ref[at + PIECE : at + 2 * PIECE, :]
        else:
            sr, si = next_ref[:PIECE, :], next_ref[PIECE:, :]
        at = x // 4 * LANES + x % 4 * PIECE
        br, bi = back[at : at + PIECE], back[at + 64 : at + 64 + PIECE]
        plain_ref[10, 2 * x : 2 * x + 2, :FULL] = over_coils(sr * br + si * bi)
        plain_ref[11, 2 * x : 2 * x + 2, :FULL] = over_coils(sr * bi - si * br)

    row = lax.broadcasted_iota(jnp.int32, (16, WIDE), 0)
    lane = lax.broadcasted_iota(jnp.int32, (16, WIDE), 1)
    known = (lane < FULL) & (row < 2 * ROWS + 2)
    inner_y = lane < FULL - 1
    inner_z = row % 2 == 0
    inner_x = row < jnp.where(last_ref[0] > 0, 2 * ROWS - 2, 16)

    def field(at):
        return jnp.where(known, plain_ref[at], 0.0)

    moved = [None] * 6
    for part in range(2):
        own, across, through = field(4 + part), field(6 + part), field(8 + part)
        masked_x = jnp.where(inner_x, own, 0.0)
        masked_y = jnp.where(inner_y, across, 0.0)
        masked_z = jnp.where(inner_z, through, 0.0)
        before = jnp.where(row < 2, field(12 + part), pltpu.roll(masked_x, 2, 0))
        adjoint = (before - masked_x) + (pltpu.roll(masked_y, 1, 1) - masked_y)
        adjoint = adjoint + (pltpu.roll(masked_z, 1, 0) - masked_z)
        now = field(part)
        new = now - 0.2 * (field(10 + part) - field(2 + part) + adjoint)
        extra = 2.0 * new - now
        grad_x = jnp.where(inner_x, pltpu.roll(extra, 14, 0) - extra, 0.0)
        grad_y = jnp.where(inner_y, pltpu.roll(extra, WIDE - 1, 1) - extra, 0.0)
        grad_z = jnp.where(inner_z, pltpu.roll(extra, 15, 0) - extra, 0.0)
        moved[part] = own + 0.5 * grad_x
        moved[2 + part] = across + 0.5 * grad_y
        moved[4 + part] = through + 0.5 * grad_z
        moved_ref[6 + part] = new
    energy = sum(value * value for value in moved)
    for channel in range(6):
        moved_ref[channel] = moved[channel]
    for copy in range(energy_ref.shape[0]):
        for t in range(3):
            energy_ref[copy, 10 * t : 10 * t + 10, :] = energy[:10, t * LANES : (t + 1) * LANES]


def last_kernel(limit, energy_ref, moved_ref, new_ref, out_ref):
    energy = energy_ref[0]
    for at in range(1, energy_ref.shape[0]):
        energy = energy + energy_ref[at]
    scale = 1.0 / jnp.maximum(1.0, jnp.sqrt(energy) / limit)
    scale = jnp.concatenate([scale[10 * t : 10 * t + 10] for t in range(3)], axis=1)
    for channel in range(6):
        value = moved_ref[channel][:10] * scale
        for x in range(ROWS):
            out_ref[0, channel, x] = value[2 * x : 2 * x + 2, :FULL]
    for part in range(2):
        for x in range(ROWS):
            new_ref[0, part, x] = moved_ref[6 + part, 2 * x : 2 * x + 2, :FULL]


PARAMS = pltpu.CompilerParams(vmem_limit_bytes=32 * 2**20)


def exchange(value):
    tiles = value.shape[0] // SLABS
    blocks = value.reshape(SLABS, 1, tiles * LANES)
    return lax.all_to_all(blocks, "slab", 0, 0, tiled=True).reshape(SLABS * tiles, LANES)


def shifted(value, axis, by):
    count = lax.axis_size(axis)
    pairs = [(i, i + by) for i in range(count) if 0 <= i + by < count]
    return lax.ppermute(value, axis, pairs)


def local(image, dual, adjoint_data, sens, kern):
    image, dual, adjoint_data, sens = (
        jnp.swapaxes(value, 2, 3) for value in (image, dual, adjoint_data, sens)
    )
    first, second, third, spread = tables()
    contrasts = lax.axis_size("con")
    weight = pl.pallas_call(
        weight_kernel,
        out_shape=jax.ShapeDtypeStruct((PADDED, WIDE), jnp.float32),
        compiler_params=PARAMS,
        name="weights",
    )(kern, spread)
    whole = pl.BlockSpec(memory_space=pltpu.HBM)
    bands = pl.pallas_call(
        first_kernel,
        in_specs=[whole] * 3,
        out_shape=jax.ShapeDtypeStruct((SLABS * TILES, LANES), jnp.float32),
        scratch_shapes=[
            pltpu.VMEM(image.shape, jnp.float32),
            pltpu.VMEM(sens.shape, jnp.float32),
            pltpu.VMEM(first.shape, jnp.bfloat16),
            pltpu.VMEM((2, WIDE, LANES), jnp.float32),
            pltpu.VMEM((2 * ROWS * PIECE, FULL), jnp.float32),
            pltpu.SemaphoreType.DMA((6,)),
        ],
        compiler_params=PARAMS,
        name="first",
    )(*(pltpu.with_memory_space_constraint(v, pltpu.HBM) for v in (image, sens, first)))
    edge, rim, sens_rows = pl.pallas_call(
        edge_kernel,
        out_shape=(
            jax.ShapeDtypeStruct((10 + 2 * COILS, 1, PLANES, FULL), jnp.float32),
            jax.ShapeDtypeStruct((2, 1, PLANES, FULL), jnp.float32),
            jax.ShapeDtypeStruct((2 * ROWS * PIECE, FULL), jnp.float32),
        ),
        compiler_params=PARAMS,
        name="edge",
    )(*(pltpu.with_memory_space_constraint(v, pltpu.HBM) for v in (image, adjoint_data, dual, sens)))
    edge = shifted(edge, "slab", -1)
    rim = shifted(rim, "slab", 1)
    is_last = (lax.axis_index("slab") == SLABS - 1).astype(jnp.int32).reshape(1)
    bands, edge, rim, is_last, sens_rows = lax.optimization_barrier(
        (exchange(bands), edge, rim, is_last, sens_rows)
    )
    returned = pl.pallas_call(
        second_kernel,
        out_shape=jax.ShapeDtypeStruct((SLABS * BACK_TILES, LANES), jnp.float32),
        compiler_params=PARAMS,
        name="second",
    )(bands, weight, second)
    moved, energy = pl.pallas_call(
        third_kernel,
        in_specs=[pl.BlockSpec(memory_space=pltpu.SMEM)]
        + [pl.BlockSpec(memory_space=pltpu.VMEM)] * 8,
        out_shape=(
            jax.ShapeDtypeStruct((8, 16, WIDE), jnp.float32),
            jax.ShapeDtypeStruct((contrasts, 30, LANES), jnp.float32),
        ),
        scratch_shapes=[
            pltpu.VMEM((2, WIDE, LANES), jnp.float32),
            pltpu.VMEM((2 * PIECE, FULL), jnp.float32),
            pltpu.VMEM((14, 16, WIDE), jnp.float32),
        ],
        compiler_params=PARAMS,
        name="third",
    )(is_last, exchange(returned), sens_rows, third, image, adjoint_data, dual, edge, rim)
    new_image, new_dual = pl.pallas_call(
        functools.partial(last_kernel, 0.9 * math.sqrt(6.0 * contrasts)),
        out_shape=(
            jax.ShapeDtypeStruct(image.shape, jnp.float32),
            jax.ShapeDtypeStruct(dual.shape, jnp.float32),
        ),
        compiler_params=PARAMS,
        name="last",
    )(lax.all_to_all(energy, "con", 0, 0, tiled=True), moved)
    return jnp.swapaxes(new_image, 2, 3), jnp.swapaxes(new_dual, 2, 3)


def solution(mesh):
    return jax.shard_map(
        local,
        mesh=mesh,
        in_specs=(
            P("con", None, None, "slab", None),
            P("con", None, None, "slab", None),
            P("con", None, None, "slab", None),
            P(None, None, None, "slab", None),
            P("con", "slab", None),
        ),
        out_specs=(P("con", None, None, "slab", None), P("con", None, None, "slab", None)),
        check_vma=False,
    )
```

```python
import functools
import math

import jax
import jax.numpy as jnp
import ml_dtypes
import numpy as np
from jax import lax
from jax.experimental import pallas as pl
from jax.experimental.pallas import tpu as pltpu
from jax.sharding import PartitionSpec as P

FULL = 320
PADDED = 640
QUARTER = 160
SLABS = 64
ROWS = 5
BAND = 10
COILS = 8
PLANES = 2
PIECE = PLANES * COILS
TILES = 13
BACK_TILES = 15
LANES = 128
WIDE = 384
PACKED = 25


def tile_of(x, b, rows):
    if b < 8:
        return 2 * x + b // 4, b % 4
    return 2 * rows + x // 2, (x % 2) * 2 + b - 8


def split(value):
    high = value.astype(jnp.bfloat16)
    return high, (value - high.astype(jnp.float32)).astype(jnp.bfloat16)


def np_split(value):
    high = value.astype(np.float32).astype(ml_dtypes.bfloat16)
    low = (value - high.astype(np.float64)).astype(np.float32).astype(ml_dtypes.bfloat16)
    return high, low


def stack_depth(value):
    high, low = np_split(value)
    return np.concatenate([high, high, low], axis=-1)


@functools.cache
def tables():
    low = np.arange(QUARTER)
    by_band = (np.arange(BAND)[:, None] + BAND * np.arange(16)[None, :]).reshape(-1)
    points_y = [4 * np.arange(80) + r for r in range(4)]
    points_x = []
    for r in range(4):
        order = [5 * (4 * u + (r - x) % 4) + x for x in range(ROWS) for u in range(16)]
        points_x.append(np.array(order))

    def stack(points, k):
        result = []
        for point in points:
            angle = 2 * np.pi * (k[:, None] * point[None, :] % PADDED) / PADDED
            result.append(np.concatenate([np.cos(angle), np.sin(angle)], axis=1))
        return np.stack(result)

    along_y = stack(points_y, by_band)
    along_x = stack(points_x, low)
    back_x = along_x.transpose(0, 2, 1)
    back_y = along_y.transpose(0, 2, 1) / PADDED**2
    spread = np.zeros((BAND, WIDE), np.float32)
    for b in range(BAND):
        for part in range(2):
            at = b // 4 * LANES + part * 64 + b % 4 * PIECE
            spread[b, at : at + PIECE] = 1.0
    first, back_y = stack_depth(along_y), stack_depth(back_y)
    second = np.stack([stack_depth(along_x), stack_depth(back_x)])
    return first, second, back_y, spread.astype(ml_dtypes.bfloat16)


def dot(left, right):
    return jnp.dot(left, right, preferred_element_type=jnp.float32)


def dot3(left, right):
    high, low = split(right)
    return dot(left, jnp.concatenate([high, low, high], axis=0))


def turn(value, shift):
    shift %= LANES
    return value if shift == 0 else pltpu.roll(value, shift, 1)


def slot_of_lane(rows):
    return lax.broadcasted_iota(jnp.int32, (rows, LANES), 1) % 64 // PIECE


def gather_pieces(sources, slots):
    result = None
    for at, source in enumerate(sources):
        if source is None:
            continue
        moved = turn(source[0], PIECE * (at - source[1]))
        result = moved if result is None else jnp.where(slots == at, moved, result)
    return result


def trade(left, right, step, slots):
    low = slots // step % 2 == 0
    shift = PIECE * step
    return jnp.where(low, left, turn(right, shift)), jnp.where(low, turn(left, -shift), right)


def transpose_pieces(tiles, slots):
    a0, a1 = trade(tiles[0], tiles[1], 1, slots)
    a2, a3 = trade(tiles[2], tiles[3], 1, slots)
    b0, b2 = trade(a0, a2, 2, slots)
    b1, b3 = trade(a1, a3, 2, slots)
    return b0, b1, b2, b3


def times_minus_i(value):
    rows = value.shape[0]
    is_real = lax.broadcasted_iota(jnp.int32, (rows, LANES), 1) < 64
    parts = []
    for at in range(0, value.shape[1], LANES):
        turned = turn(value[:, at : at + LANES], 64)
        parts.append(jnp.where(is_real, turned, -turned))
    return jnp.concatenate(parts, axis=1)


def butterfly(a0, a1, a2, a3):
    even, odd = a0 + a2, a1 + a3
    apart, turned = a0 - a2, times_minus_i(a1 - a3)
    return even + odd, apart + turned, even - odd, apart - turned


def forward(table, residues):
    parts = []
    for r in range(4):
        data = jnp.concatenate([residues[r], times_minus_i(residues[r])], axis=0)
        parts.append(dot3(table[r], data))
    return butterfly(*parts)


def backward(table, quarters):
    sums = butterfly(*quarters)
    result = []
    for r, at in enumerate((0, 3, 2, 1)):
        both = dot3(table[r], sums[at])
        result.append(both[:80] - times_minus_i(both[80:]))
    return result


def gather_rows(sens_ref, rows_ref):
    for x in range(ROWS):
        for part in range(2):
            for j in range(COILS):
                row = (2 * x + part) * PIECE + 2 * j
                rows_ref[row : row + 2, :] = sens_ref[j, part, x]


def first_kernel(
    image_hbm, sens_hbm, table_hbm, out_ref,
    image_ref, sens_ref, table_ref, flat_ref, rows_ref, sems,
):
    copies = [
        pltpu.make_async_copy(sens_hbm, sens_ref, sems.at[0]),
        pltpu.make_async_copy(image_hbm, image_ref, sems.at[1]),
    ]
    for r in range(4):
        copies.append(pltpu.make_async_copy(table_hbm.at[r], table_ref.at[r], sems.at[2 + r]))
    for copy in copies:
        copy.start()
    copies[0].wait()
    gather_rows(sens_ref, rows_ref)
    copies[1].wait()
    real, imag = [], []
    for x in range(ROWS):
        sr = rows_ref[2 * x * PIECE : (2 * x + 1) * PIECE, :]
        si = rows_ref[(2 * x + 1) * PIECE : (2 * x + 2) * PIECE, :]
        ur = jnp.concatenate([image_ref[0, 0, x]] * COILS, axis=0)
        ui = jnp.concatenate([image_ref[0, 1, x]] * COILS, axis=0)
        real.append(sr * ur - si * ui)
        imag.append(sr * ui + si * ur)
    rest = [jnp.zeros((3 * PIECE, FULL), jnp.float32)]
    coil = jnp.concatenate(real[:4] + imag[:4] + real[4:] + rest + imag[4:] + rest, axis=0)
    coil = jnp.concatenate([coil, jnp.zeros((256, WIDE - FULL), jnp.float32)], axis=1).T
    flat_ref[0] = coil[:, :LANES]
    flat_ref[1] = coil[:, LANES:]
    residues = []
    for r in range(4):
        columns = [flat_ref[column, pl.ds(r, 80, stride=4), :] for column in range(2)]
        residues.append(jnp.concatenate(columns, axis=1))

    for r in range(4):
        copies[2 + r].wait()
    bands = forward(table_ref, residues)
    slots = slot_of_lane(16)
    for q in range(4):
        start = 16 * q * TILES

        def put(t, value):
            out_ref[pl.ds(start + t, 16, stride=TILES), :] = value

        near = [bands[q][b * 16 : (b + 1) * 16, :LANES] for b in range(BAND)]
        far = [bands[q][b * 16 : (b + 1) * 16, LANES:] for b in range(BAND)]
        for g in range(2):
            for x, value in enumerate(transpose_pieces(near[4 * g : 4 * g + 4], slots)):
                put(2 * x + g, value)
            put(8 + g, gather_pieces([(far[4 * g + i], 0) for i in range(4)], slots))
        for pair, value in enumerate(trade(*trade(near[8], near[9], 1, slots), 2, slots)):
            put(10 + pair, value)
        put(12, gather_pieces([(far[8], 0), (far[9], 0)], slots))


def weight_kernel(kern_ref, spread_ref, out_ref):
    form = (((0,), (0,)), ((), ()))
    high, low = split(kern_ref[0])
    out_ref[...] = lax.dot_general(
        high, spread_ref[...], form, preferred_element_type=jnp.float32
    ) + lax.dot_general(low, spread_ref[...], form, preferred_element_type=jnp.float32)


def edge_kernel(image_ref, measured_ref, dual_ref, sens_ref, edge_ref, rim_ref, rows_ref):
    gather_rows(sens_ref, rows_ref)
    for at, count, source in ((0, 2, image_ref), (2, 2, measured_ref), (4, 6, dual_ref)):
        for channel in range(count):
            edge_ref[at + channel, 0] = source[0, channel, 0]
    for j in range(COILS):
        for part in range(2):
            edge_ref[10 + 2 * j + part, 0] = sens_ref[j, part, 0]
    for part in range(2):
        rim_ref[part, 0] = dual_ref[0, part, ROWS - 1]


def second_kernel(in_ref, weight_ref, table_ref, out_ref):
    def place(x, r, t):
        return pl.ds((r - x) % 4 * TILES + t, 16, stride=4 * TILES)

    residues = []
    for r in range(4):
        rows = []
        for x in range(ROWS):
            rest = turn(in_ref[place(x, r, 10 + x // 2), :], -2 * PIECE * (x % 2))
            whole = [in_ref[place(x, r, 2 * x), :], in_ref[place(x, r, 2 * x + 1), :]]
            rows.append(jnp.concatenate(whole + [rest], axis=1))
        residues.append(jnp.concatenate(rows, axis=0))
    spectrum = forward(table_ref.at[0], residues)
    weighted = [
        part * weight_ref[q * QUARTER : (q + 1) * QUARTER, :] for q, part in enumerate(spectrum)
    ]
    result = backward(table_ref.at[1], weighted)
    lower = slot_of_lane(16) < 2
    for s in range(4):

        def put(t, value):
            out_ref[pl.ds(s * BACK_TILES + t, 16, stride=4 * BACK_TILES), :] = value

        rows = [result[(s + x) % 4][x * 16 : (x + 1) * 16] for x in range(ROWS)]
        following = result[(s + 1) % 4][:16]
        rows.append(pltpu.roll(following, 15, 0) if s == 3 else following)
        for x in range(ROWS + 1):
            for g in range(2):
                put(2 * x + g, rows[x][:, g * LANES : (g + 1) * LANES])
        for pair in range(3):
            left, right = rows[2 * pair][:, 2 * LANES :], rows[2 * pair + 1][:, 2 * LANES :]
            put(12 + pair, jnp.where(lower, left, turn(right, 2 * PIECE)))


def third_kernel(
    last_ref, in_ref, rows_ref, table_ref, image_ref, measured_ref, dual_ref, edge_ref, rim_ref,
    moved_ref, energy_ref, flat_ref, next_ref, plain_ref,
):
    slots = slot_of_lane(16)
    quarters = []
    for q in range(4):
        start = 16 * q * BACK_TILES
        tiles = [in_ref[pl.ds(start + t, 16, stride=BACK_TILES), :] for t in range(BACK_TILES)]
        near, far = [], []
        for g in range(2):
            near += transpose_pieces([tiles[2 * x + g] for x in range(4)], slots)
            pairs = trade(tiles[8 + g], tiles[10 + g], 1, slots)
            far += [*pairs, *(turn(value, -2 * PIECE) for value in pairs)]
        near += trade(*trade(tiles[12], tiles[13], 2, slots), 1, slots)
        far += trade(tiles[14], turn(tiles[14], -2 * PIECE), 1, slots)
        columns = [jnp.concatenate(near, axis=0), jnp.concatenate(far, axis=0)]
        quarters.append(jnp.concatenate(columns, axis=1))
    back = backward(table_ref, quarters)
    flat_ref[:, FULL:, :] = jnp.zeros((2, WIDE - FULL, LANES), jnp.float32)
    for r in range(4):
        for column in range(2):
            flat_ref[column, pl.ds(r, 80, stride=4), :] = back[r][
                :, column * LANES : (column + 1) * LANES
            ]
    back = jnp.concatenate([flat_ref[0].T, flat_ref[1].T], axis=0)[:, :FULL]

    def over_coils(value):
        half = value[:8] + value[8:]
        quarter = half[:4] + half[4:]
        return quarter[:2] + quarter[2:]

    for part in range(2):
        plain_ref[12 + part, :2, :FULL] = rim_ref[part, 0]
        for j in range(COILS):
            row = part * PIECE + 2 * j
            next_ref[row : row + 2, :] = edge_ref[10 + 2 * j + part, 0]
    for source, at, count in ((image_ref, 0, 2), (measured_ref, 2, 2), (dual_ref, 4, 6)):
        for channel in range(count):
            for x in range(ROWS):
                plain_ref[at + channel, 2 * x : 2 * x + 2, :FULL] = source[0, channel, x]
            plain_ref[at + channel, 2 * ROWS : 2 * ROWS + 2, :FULL] = edge_ref[at + channel, 0]
    for x in range(ROWS + 1):
        if x < ROWS:
            at = 2 * x * PIECE
            sr, si = rows_ref[at : at + PIECE, :], rows_ref[at + PIECE : at + 2 * PIECE, :]
        else:
            sr, si = next_ref[:PIECE, :], next_ref[PIECE:, :]
        at = x // 4 * LANES + x % 4 * PIECE
        br, bi = back[at : at + PIECE], back[at + 64 : at + 64 + PIECE]
        plain_ref[10, 2 * x : 2 * x + 2, :FULL] = over_coils(sr * br + si * bi)
        plain_ref[11, 2 * x : 2 * x + 2, :FULL] = over_coils(sr * bi - si * br)

    row = lax.broadcasted_iota(jnp.int32, (16, WIDE), 0)
    lane = lax.broadcasted_iota(jnp.int32, (16, WIDE), 1)
    known = (lane < FULL) & (row < 2 * ROWS + 2)
    inner_y = lane < FULL - 1
    inner_z = row % 2 == 0
    inner_x = row < jnp.where(last_ref[0] > 0, 2 * ROWS - 2, 16)

    def field(at):
        return jnp.where(known, plain_ref[at], 0.0)

    moved = [None] * 6
    for part in range(2):
        own, across, through = field(4 + part), field(6 + part), field(8 + part)
        masked_x = jnp.where(inner_x, own, 0.0)
        masked_y = jnp.where(inner_y, across, 0.0)
        masked_z = jnp.where(inner_z, through, 0.0)
        before = jnp.where(row < 2, field(12 + part), pltpu.roll(masked_x, 2, 0))
        adjoint = (before - masked_x) + (pltpu.roll(masked_y, 1, 1) - masked_y)
        adjoint = adjoint + (pltpu.roll(masked_z, 1, 0) - masked_z)
        now = field(part)
        new = now - 0.2 * (field(10 + part) - field(2 + part) + adjoint)
        extra = 2.0 * new - now
        grad_x = jnp.where(inner_x, pltpu.roll(extra, 14, 0) - extra, 0.0)
        grad_y = jnp.where(inner_y, pltpu.roll(extra, WIDE - 1, 1) - extra, 0.0)
        grad_z = jnp.where(inner_z, pltpu.roll(extra, 15, 0) - extra, 0.0)
        moved[part] = own + 0.5 * grad_x
        moved[2 + part] = across + 0.5 * grad_y
        moved[4 + part] = through + 0.5 * grad_z
        moved_ref[6 + part] = new
    energy = sum(value * value for value in moved)
    for channel in range(6):
        moved_ref[channel] = moved[channel]
    rest = energy[:, 2 * LANES :]
    rest = jnp.where(lane[:5, :LANES] < 64, rest[:5], turn(rest, 64)[5:10])
    packed = jnp.concatenate([energy[:10, :LANES], energy[:10, LANES : 2 * LANES], rest], axis=0)
    for at in range(0, energy_ref.shape[0], PACKED):
        energy_ref[at : at + PACKED, :] = packed


def last_kernel(limit, energy_ref, moved_ref, new_ref, out_ref):
    energy = energy_ref[:PACKED, :]
    for at in range(PACKED, energy_ref.shape[0], PACKED):
        energy = energy + energy_ref[at : at + PACKED, :]
    scale = 1.0 / jnp.maximum(1.0, jnp.sqrt(energy) / limit)
    rest = jnp.concatenate([scale[20:], turn(scale[20:], 64)], axis=0)
    scale = jnp.concatenate([scale[:10], scale[10:20], rest], axis=1)
    for channel in range(6):
        value = moved_ref[channel][:10] * scale
        for x in range(ROWS):
            out_ref[0, channel, x] = value[2 * x : 2 * x + 2, :FULL]
    for part in range(2):
        for x in range(ROWS):
            new_ref[0, part, x] = moved_ref[6 + part, 2 * x : 2 * x + 2, :FULL]


PARAMS = pltpu.CompilerParams(vmem_limit_bytes=32 * 2**20)


def exchange(value, axis, count):
    blocks = value.reshape(count, 1, -1)
    return lax.all_to_all(blocks, axis, 0, 0, tiled=True).reshape(value.shape)


def shifted(value, axis, by):
    count = lax.axis_size(axis)
    pairs = [(i, i + by) for i in range(count) if 0 <= i + by < count]
    return lax.ppermute(value, axis, pairs)


def local(image, dual, adjoint_data, sens, kern):
    image, dual, adjoint_data, sens = (
        jnp.swapaxes(value, 2, 3) for value in (image, dual, adjoint_data, sens)
    )
    first, second, third, spread = tables()
    contrasts = lax.axis_size("con")
    weight = pl.pallas_call(
        weight_kernel,
        out_shape=jax.ShapeDtypeStruct((PADDED, WIDE), jnp.float32),
        compiler_params=PARAMS,
        name="weights",
    )(kern, spread)
    whole = pl.BlockSpec(memory_space=pltpu.HBM)
    bands = pl.pallas_call(
        first_kernel,
        in_specs=[whole] * 3,
        out_shape=jax.ShapeDtypeStruct((SLABS * TILES, LANES), jnp.float32),
        scratch_shapes=[
            pltpu.VMEM(image.shape, jnp.float32),
            pltpu.VMEM(sens.shape, jnp.float32),
            pltpu.VMEM(first.shape, jnp.bfloat16),
            pltpu.VMEM((2, WIDE, LANES), jnp.float32),
            pltpu.VMEM((2 * ROWS * PIECE, FULL), jnp.float32),
            pltpu.SemaphoreType.DMA((6,)),
        ],
        compiler_params=PARAMS,
        name="first",
    )(*(pltpu.with_memory_space_constraint(v, pltpu.HBM) for v in (image, sens, first)))
    edge, rim, sens_rows = pl.pallas_call(
        edge_kernel,
        out_shape=(
            jax.ShapeDtypeStruct((10 + 2 * COILS, 1, PLANES, FULL), jnp.float32),
            jax.ShapeDtypeStruct((2, 1, PLANES, FULL), jnp.float32),
            jax.ShapeDtypeStruct((2 * ROWS * PIECE, FULL), jnp.float32),
        ),
        compiler_params=PARAMS,
        name="edge",
    )(*(pltpu.with_memory_space_constraint(v, pltpu.HBM) for v in (image, adjoint_data, dual, sens)))
    edge = shifted(edge, "slab", -1)
    rim = shifted(rim, "slab", 1)
    is_last = (lax.axis_index("slab") == SLABS - 1).astype(jnp.int32).reshape(1)
    bands, edge, rim, is_last, sens_rows = lax.optimization_barrier(
        (exchange(bands, "slab", SLABS), edge, rim, is_last, sens_rows)
    )
    returned = pl.pallas_call(
        second_kernel,
        out_shape=jax.ShapeDtypeStruct((SLABS * BACK_TILES, LANES), jnp.float32),
        compiler_params=PARAMS,
        name="second",
    )(bands, weight, second)
    moved, energy = pl.pallas_call(
        third_kernel,
        in_specs=[pl.BlockSpec(memory_space=pltpu.SMEM)]
        + [pl.BlockSpec(memory_space=pltpu.VMEM)] * 8,
        out_shape=(
            jax.ShapeDtypeStruct((8, 16, WIDE), jnp.float32),
            jax.ShapeDtypeStruct((contrasts * PACKED, LANES), jnp.float32),
        ),
        scratch_shapes=[
            pltpu.VMEM((2, WIDE, LANES), jnp.float32),
            pltpu.VMEM((2 * PIECE, FULL), jnp.float32),
            pltpu.VMEM((14, 16, WIDE), jnp.float32),
        ],
        compiler_params=PARAMS,
        name="third",
    )(is_last, exchange(returned, "slab", SLABS), sens_rows, third, image, adjoint_data, dual, edge, rim)
    new_image, new_dual = pl.pallas_call(
        functools.partial(last_kernel, 0.9 * math.sqrt(6.0 * contrasts)),
        out_shape=(
            jax.ShapeDtypeStruct(image.shape, jnp.float32),
            jax.ShapeDtypeStruct(dual.shape, jnp.float32),
        ),
        compiler_params=PARAMS,
        name="last",
    )(exchange(energy, "con", contrasts), moved)
    return jnp.swapaxes(new_image, 2, 3), jnp.swapaxes(new_dual, 2, 3)


def solution(mesh):
    return jax.shard_map(
        local,
        mesh=mesh,
        in_specs=(
            P("con", None, None, "slab", None),
            P("con", None, None, "slab", None),
            P("con", None, None, "slab", None),
            P(None, None, None, "slab", None),
            P("con", "slab", None),
        ),
        out_specs=(P("con", None, None, "slab", None), P("con", None, None, "slab", None)),
        check_vma=False,
    )
```
